32 devices in a mesh: groups: 2 (over y), space: 8 (over z, x), heads: 2 (over core).
Axes of the slice: x: 2, y: 2, z: 4, core: 2. Of those that a mesh axis runs over, the one named last changes fastest.
Arguments:
- queries: bfloat16 [2400, 1536], P(('groups', 'space'), 'heads'), parts along dimension 0, may hold values from -16 to 16
- latent_keys: bfloat16 [2400, 1536], P(('groups', 'space'), 'heads'), parts along dimension 0, may hold values from -9 to 9
- latent_values: bfloat16 [2400, 1536], P(('groups', 'space'), 'heads'), parts along dimension 0, may hold values from -6 to 6
- prompt: bfloat16 [512, 3072], P('groups'), parts along dimension 0, may hold values from -44 to 44
- key_weight: bfloat16 [3072, 1536], P('space', 'heads'), may hold values from -0.15625 to 0.15625
- value_weight: bfloat16 [3072, 1536], P('space', 'heads'), may hold values from -0.15625 to 0.15625
- out_weight: bfloat16 [1536, 3072], P('heads', 'space'), may hold values from -0.21875 to 0.21875
- tile_owner: int32 [16], P('groups'), parts along dimension 0, may hold values from 0 to 7, as said below
Outputs:
- block_output: bfloat16 [2400, 3072], P(('groups', 'space'), 'heads'), parts along dimension 0
The draws below stay inside these ranges and needn't reach their ends.
There are 2 independent parts, one for each index of `groups`. The reference program is written for one: setup_inputs(seed, part) draws one part's arguments, and reference() takes and returns one part's arrays. A program takes and returns all parts, laid end to end along the dimension named above; an argument that names none is the same for every part. Nothing has to cross between parts.
Inputs may be any that keep to these rules, and one draw needn't show every extreme that they name: `tile_owner`: tile t = i * 2 + j of the 4 x 2 grid is held by slot a * 2 + b, with a = (i + r) mod 4 or a = (3 - i + r) mod 4 for one r, and b = j or b = 1 - j; r and each of the two alternatives are the same for all tiles.
All inputs are finite; a program needn't handle non-finite values.
Results may differ from the reference program's by a relative error of at most 0.0081.
Values may be sent and summed in bfloat16 or wider, within the bound.
A program may use at most 64 MiB of HBM per device.

```python
import jax
import jax.numpy as jnp
from jax import lax

D = 3072
HD = 128
HEADS = 12
RT = 16
RH = 56
TEXT = 256
TILE = 5
GH = 4
GW = 2
TOK = 150
LATENT = 1200
N_SPACE = 8
N_HEADS = 2


def draw_queries(key, part):
    drawn_draw = jnp.clip(jax.random.normal(jax.random.fold_in(key, 1), (LATENT, HEADS * HD), jnp.float32), -6.0, 6.0)
    return drawn_draw.astype(jnp.bfloat16)


def draw_latent_keys(key, part):
    drawn_draw = jnp.clip(jax.random.normal(jax.random.fold_in(key, 2), (LATENT, HEADS * HD), jnp.float32), -6.0, 6.0)
    return drawn_draw.astype(jnp.bfloat16)


def draw_prompt(key, part):
    scale_draw = jax.random.uniform(jax.random.fold_in(key, 3), (TEXT, 1), jnp.float32)
    drawn_draw = jnp.clip(jax.random.normal(jax.random.fold_in(key, 6), (TEXT, D), jnp.float32), -4.0, 4.0)
    row_scale = 10.0 ** scale_draw
    return (drawn_draw * row_scale).astype(jnp.bfloat16)


def draw_tile_owner(key, part):
    flip_bits = jax.random.randint(jax.random.fold_in(key, 11), (2,), 0, 2)
    offset = jax.random.randint(jax.random.fold_in(key, 12), (), 0, GH)
    tile_index = jnp.arange(GH * GW, dtype=jnp.int32)
    tile_row = tile_index // GW
    tile_col = tile_index % GW
    tile_row = jnp.where(flip_bits[0] == 1, GH - 1 - tile_row, tile_row)
    tile_row = (tile_row + offset) % GH
    tile_col = jnp.where(flip_bits[1] == 1, GW - 1 - tile_col, tile_col)
    return (tile_row * GW + tile_col).astype(jnp.int32)


def spiked(drawn, rng, source, target, parts, factor):
    owner, partner = [(jnp.arange(drawn.shape[position]) // (drawn.shape[position] // parts)).reshape([-1 if axis == position else 1 for axis in range(drawn.ndim)]) for position in (source, target)]
    chosen = jax.random.permutation(rng, parts)[partner]
    strong = (owner == chosen) | (owner == (partner + parts // 2) % parts)
    return jnp.where(strong, factor * drawn, drawn)


def steps_of(key, shape, shards, low, top_value):
    loudness = 1.0
    for position, shards_of in shards:
        steps = jax.random.uniform(jax.random.fold_in(jax.random.fold_in(key, 6), position), (shards_of,), jnp.float32, low / len(shards), top_value / len(shards))
        loudness = loudness * jnp.repeat(jnp.exp(steps), shape[position] // shards_of).reshape((-1,) + (1,) * (len(shape) - 1 - position))
    return loudness


def bell_draw(rng, dims, spread, bound, cuts=(), kind=jnp.bfloat16):
    array = spread * jax.random.normal(rng, dims, jnp.float32)
    if cuts:
        array = array * steps_of(rng, dims, cuts, -0.22, 0.18)
    return jnp.clip(array, -bound, bound).astype(kind)


def gaussian_with(key, extent, deviation, most, split, heavy, held_as=jnp.bfloat16):
    array = deviation * jax.random.normal(key, extent, jnp.float32)
    if split:
        array = array * steps_of(key, extent, split, -0.22, 0.18)
    return jnp.clip(spiked(array, jax.random.fold_in(key, 3), *heavy), -most, most).astype(held_as)


def setup_inputs(seed: int = 0, part: int = 0) -> dict:
    key_of = jax.random.split(jax.random.key(seed), 9)
    part_splits = jax.random.split(jax.random.fold_in(key_of[8], part), 9)
    return {
        "queries": draw_queries(jax.random.fold_in(jax.random.fold_in(key_of[8], part), 71), part),
        "latent_keys": draw_latent_keys(jax.random.fold_in(jax.random.fold_in(key_of[8], part), 71), part),
        "latent_values": bell_draw(part_splits[2], (LATENT, HEADS * HD), 1.0, 6.0, ((0, 8), (1, 2))),
        "prompt": draw_prompt(jax.random.fold_in(jax.random.fold_in(key_of[8], part), 71), part),
        "key_weight": gaussian_with(key_of[4], (D, HEADS * HD), D ** -0.5, 0.15625, ((0, 8), (1, 2)), (0, 1, 8, 2.0)),
        "value_weight": gaussian_with(key_of[5], (D, HEADS * HD), D ** -0.5, 0.15625, ((0, 8), (1, 2)), (0, 1, 8, 2.0)),
        "out_weight": gaussian_with(key_of[6], (HEADS * HD, D), (HEADS * HD) ** -0.5, 0.21875, ((0, 2), (1, 8)), (0, 1, 8, 2.0)),
        "tile_owner": draw_tile_owner(jax.random.fold_in(jax.random.fold_in(key_of[8], part), 71), part),
    }


rope_theta = 256.0
eps_norm = 1e-06
masked_score = -1e+30

def rope_tables(frame_pos, height_pos, width_pos):
    pairs_time = jnp.arange(RT // 2, dtype=jnp.float32)
    pairs_space = jnp.arange(RH // 2, dtype=jnp.float32)
    freq_time = rope_theta ** (-2.0 * pairs_time / RT)
    freq_space = rope_theta ** (-2.0 * pairs_space / RH)
    angles = jnp.concatenate([frame_pos[:, None] * freq_time[None, :], height_pos[:, None] * freq_space[None, :], width_pos[:, None] * freq_space[None, :]], axis=1)
    return (jnp.cos(angles), jnp.sin(angles))

def rotate(stacked, cosine, sine_table):
    row_count = stacked.shape[0]
    head_total = stacked.shape[1]
    paired = stacked.reshape(row_count, head_total, HD // 2, 2)
    even_part = paired[..., 0]
    odd_part = paired[..., 1]
    cos_rows = cosine[:, None, :]
    sin_rows = sine_table[:, None, :]
    turned = jnp.stack([even_part * cos_rows - odd_part * sin_rows, even_part * sin_rows + odd_part * cos_rows], axis=-1)
    return turned.reshape(row_count, head_total * HD)

def normalize_keys(summed, head_total):
    row_count = summed.shape[0]
    half_width = summed.shape[1] // 2
    key_part = summed[:, :half_width].reshape(row_count, head_total, HD)
    key_part = key_part * lax.rsqrt(lax.optimization_barrier(jnp.mean(key_part * key_part, axis=-1, keepdims=True)) + eps_norm)
    return jnp.concatenate([key_part.reshape(row_count, half_width), summed[:, half_width:]], axis=1).astype(jnp.bfloat16)

def reference(queries, latent_keys, latent_values, prompt, key_weight, value_weight, out_weight, tile_owner):
    head_width = HEADS * HD
    slot_index = jnp.arange(N_SPACE, dtype=jnp.int32)
    tile_of_slot = jnp.zeros((N_SPACE,), jnp.int32).at[tile_owner].set(slot_index)
    row_index = jnp.arange(LATENT, dtype=jnp.int32)
    slot_of_row = row_index // TOK
    cell_index = row_index % TOK
    tile_index = tile_of_slot[slot_of_row]
    frame_pos = (cell_index // (TILE * TILE)).astype(jnp.float32)
    height_pos = (tile_index // GW * TILE + cell_index // TILE % TILE).astype(jnp.float32)
    width_pos = (tile_index % GW * TILE + cell_index % TILE).astype(jnp.float32)
    cosine, sine_table = rope_tables(frame_pos, height_pos, width_pos)
    query_rot = rotate(queries.astype(jnp.float32).reshape(LATENT, HEADS, HD), cosine, sine_table).astype(jnp.bfloat16)
    key_rot = rotate(latent_keys.astype(jnp.float32).reshape(LATENT, HEADS, HD), cosine, sine_table).astype(jnp.bfloat16)
    query_rot = lax.optimization_barrier(query_rot)
    text_sum = jnp.dot(prompt, jnp.concatenate([key_weight, value_weight], axis=1), preferred_element_type=jnp.float32)
    text_kv = lax.optimization_barrier(normalize_keys(text_sum, HEADS))
    kv_all = jnp.concatenate([key_rot, latent_values], axis=1).reshape(N_SPACE, TOK, 2 * head_width)
    kv_all = lax.optimization_barrier(kv_all)

    def one_slot(slot):
        tile_here = tile_of_slot[slot]
        tile_row = tile_here // GW
        tile_col = tile_here % GW
        gathered = []
        valid_parts = []
        for row_step in (-1, 0, 1):
            for col_step in (-1, 0, 1):
                near_row = tile_row + row_step
                near_col = tile_col + col_step
                inside = (near_row >= 0) & (near_row < GH) & (near_col >= 0) & (near_col < GW)
                near_tile = jnp.clip(near_row, 0, GH - 1) * GW + jnp.clip(near_col, 0, GW - 1)
                gathered.append(kv_all[tile_owner[near_tile]])
                valid_parts.append(jnp.zeros((TOK,), jnp.int32) + inside.astype(jnp.int32))
        gathered.append(text_kv)
        valid_parts.append(jnp.ones((TEXT,), jnp.int32))
        keys_all = jnp.concatenate(gathered, axis=0)
        key_valid = jnp.concatenate(valid_parts, axis=0)
        query_here = lax.dynamic_slice_in_dim(query_rot, (slot * TOK).astype(jnp.int32), TOK, 0)
        query_heads = query_here.astype(jnp.float32).reshape(TOK, HEADS, HD)
        key_heads = keys_all[:, :head_width].astype(jnp.float32).reshape(-1, HEADS, HD)
        value_heads = keys_all[:, head_width:].astype(jnp.float32).reshape(-1, HEADS, HD)
        scores = jnp.einsum('qhd,khd->hqk', query_heads, key_heads) * HD ** (-0.5)
        scores = jnp.where(key_valid[None, None, :] > 0, scores, masked_score)
        top_score = lax.optimization_barrier(jnp.max(scores, axis=-1, keepdims=True))
        exponent = jnp.exp(scores - top_score)
        weights = (exponent / lax.optimization_barrier(jnp.sum(exponent, axis=-1, keepdims=True))).astype(jnp.bfloat16)
        weights = lax.optimization_barrier(weights)
        attended = jnp.einsum('hqk,khd->qhd', weights.astype(jnp.float32), value_heads)
        return attended.reshape(TOK, head_width).astype(jnp.bfloat16)
    attended_all = lax.map(one_slot, slot_index).reshape(LATENT, head_width)
    group_rows = head_width // N_HEADS
    summed_out = jnp.zeros((LATENT, D), jnp.float32)
    for group_index in range(N_HEADS):
        lower = group_index * group_rows
        partial_value = jnp.dot(attended_all[:, lower:lower + group_rows], out_weight[lower:lower + group_rows], preferred_element_type=jnp.float32)
        summed_out = summed_out + lax.optimization_barrier(partial_value.astype(jnp.bfloat16)).astype(jnp.float32)
    return summed_out.astype(jnp.bfloat16)
```

```python
import functools

import jax
import jax.numpy as jnp
import numpy as np
from jax import lax
from jax.experimental import pallas as pl
from jax.experimental.pallas import tpu as pltpu
from jax.sharding import PartitionSpec as P

HD = 128
RT = 16
RH = 56
TILE = 5


rope_theta = 256.0
eps_norm = 1e-06
masked_score = -1e30


def shifted(value, axis, steps):
    count = lax.axis_size(axis)
    pairs = [(source, (source + steps) % count) for source in range(count)]
    return lax.ppermute(value, axis, pairs)


def rope_tables(frame_pos, height_pos, width_pos):
    pairs_time = jnp.arange(RT // 2, dtype=jnp.float32)
    pairs_space = jnp.arange(RH // 2, dtype=jnp.float32)
    freq_time = rope_theta ** (-2.0 * pairs_time / RT)
    freq_space = rope_theta ** (-2.0 * pairs_space / RH)
    angles = jnp.concatenate(
        [
            frame_pos[:, None] * freq_time[None, :],
            height_pos[:, None] * freq_space[None, :],
            width_pos[:, None] * freq_space[None, :],
        ],
        axis=1,
    )
    return (jnp.cos(angles), jnp.sin(angles))


def rotate(stacked, cosine, sine_table):
    row_count = stacked.shape[0]
    head_total = stacked.shape[1]
    paired = stacked.reshape(row_count, head_total, HD // 2, 2)
    even_part = paired[..., 0]
    odd_part = paired[..., 1]
    cos_rows = cosine[:, None, :]
    sin_rows = sine_table[:, None, :]
    turned = jnp.stack(
        [even_part * cos_rows - odd_part * sin_rows, even_part * sin_rows + odd_part * cos_rows],
        axis=-1,
    )
    return turned.reshape(row_count, head_total * HD)


def normalize_keys(summed, head_total):
    row_count = summed.shape[0]
    half_width = summed.shape[1] // 2
    key_part = summed[:, :half_width].reshape(row_count, head_total, HD)
    key_part = key_part * lax.rsqrt(
        jnp.mean(key_part * key_part, axis=-1, keepdims=True) + eps_norm
    )
    return jnp.concatenate(
        [key_part.reshape(row_count, half_width), summed[:, half_width:]], axis=1
    ).astype(jnp.bfloat16)


def body(
    queries, latent_keys, latent_values, prompt, key_weight, value_weight, out_weight, tile_owner
):
    spaces = lax.axis_size("space")
    device = lax.axis_index("space")
    grid_h = min(8, spaces // 2)
    grid_w = spaces // grid_h
    tok_rows = queries.shape[0]
    head_width = queries.shape[1]
    head_count = head_width // HD
    tile_total = tile_owner.shape[0]
    tile_index = jnp.arange(tile_total, dtype=jnp.int32)
    own_tile = jnp.sum(jnp.where(tile_owner == device, tile_index, 0))
    tile_row = own_tile // grid_w
    tile_col = own_tile % grid_w
    anchor_slot = tile_owner[0]
    right_slot = tile_owner[min(1, tile_total - 1)]
    lower_slot = tile_owner[min(grid_w, tile_total - 1)]
    col_sign = jnp.where(right_slot % grid_w - anchor_slot % grid_w == -1, -1, 1)
    row_sign = jnp.where((lower_slot // grid_w - anchor_slot // grid_w) % grid_h == 1, 1, -1)
    cell_index = jnp.arange(tok_rows, dtype=jnp.int32)
    frame_pos = (cell_index // (TILE * TILE)).astype(jnp.float32)
    height_pos = (tile_row * TILE + cell_index // TILE % TILE).astype(jnp.float32)
    width_pos = (tile_col * TILE + cell_index % TILE).astype(jnp.float32)
    cosine, sine_table = rope_tables(frame_pos, height_pos, width_pos)
    query_rot = rotate(
        queries.astype(jnp.float32).reshape(tok_rows, head_count, HD), cosine, sine_table
    ).astype(jnp.bfloat16)
    key_rot = rotate(
        latent_keys.astype(jnp.float32).reshape(tok_rows, head_count, HD), cosine, sine_table
    ).astype(jnp.bfloat16)
    width_rows = key_weight.shape[0]
    text_cols = lax.dynamic_slice_in_dim(prompt, device * width_rows, width_rows, 1)
    both_weights = jnp.concatenate([key_weight, value_weight], axis=1)
    partial_text = jnp.dot(text_cols, both_weights, preferred_element_type=jnp.float32)
    summed_text = lax.psum(partial_text, "space")
    text_kv = normalize_keys(summed_text, head_count)
    kv_own = jnp.concatenate([key_rot, latent_values], axis=1)
    blocks = []
    valid_parts = []
    for row_step in (-1, 0, 1):
        for col_step in (-1, 0, 1):
            if row_step == 0 and col_step == 0:
                fetched = kv_own
            else:
                fetched = shifted(kv_own, "space", -(row_step * grid_w + col_step))
            near_row = tile_row + row_sign * row_step
            near_col = tile_col + col_sign * col_step
            inside = (near_row >= 0) & (near_row < grid_h) & (near_col >= 0) & (near_col < grid_w)
            blocks.append(fetched)
            valid_parts.append(jnp.zeros((tok_rows,), jnp.int32) + inside.astype(jnp.int32))
    blocks.append(text_kv)
    valid_parts.append(jnp.ones((text_kv.shape[0],), jnp.int32))
    keys_all = jnp.concatenate(blocks, axis=0)
    key_valid = jnp.concatenate(valid_parts, axis=0)
    score_scale = HD ** (-0.5)
    head_outputs = []
    for head_index in range(head_count):
        head_start = head_index * HD
        query_slice = query_rot[:, head_start : head_start + HD]
        key_slice = keys_all[:, head_start : head_start + HD]
        value_slice = keys_all[:, head_width + head_start : head_width + head_start + HD]
        scores = (
            lax.dot_general(
                query_slice, key_slice, (((1,), (1,)), ((), ())), preferred_element_type=jnp.float32
            )
            * score_scale
        )
        scores = jnp.where(key_valid[None, :] > 0, scores, masked_score)
        top_score = jnp.max(scores, axis=-1, keepdims=True)
        exponent = jnp.exp(scores - top_score)
        weights = (exponent / jnp.sum(exponent, axis=-1, keepdims=True)).astype(jnp.bfloat16)
        head_outputs.append(
            jnp.dot(weights, value_slice, preferred_element_type=jnp.float32).astype(jnp.bfloat16)
        )
    attended = jnp.concatenate(head_outputs, axis=1)
    partial_out = jnp.dot(
        attended,
        lax.all_gather(out_weight, "space", axis=1, tiled=True),
        preferred_element_type=jnp.float32,
    )
    summed_out = lax.psum_scatter(
        partial_out.astype(jnp.bfloat16), "heads", scatter_dimension=1, tiled=True
    )
    return summed_out


MESH = pl.DeviceIdType.MESH


def mult(value, step):
    return pl.multiple_of(value, step)


def fused_kernel(
    rows,
    head_count,
    rope_ref,
    bias_ref,
    qkv_ref,
    prompt_ref,
    kw_ref,
    vw_ref,
    ow_ref,
    out_ref,
    tcols,
    xs_q,
    xs_kv,
    qbuf,
    kv,
    txs,
    txr,
    tsum,
    rss,
    rsr,
    att_s,
    att,
    wbuf,
    part_s,
    part_r,
    local_sem,
    send_sem,
    recv_sem,
):
    g = lax.axis_index("groups")
    s = lax.axis_index("space")
    h = lax.axis_index("heads")
    a, b = s // 2, s % 2
    other = 1 - b
    half = head_count // 2
    width = half * HD
    full = head_count * HD
    x_peer = {"space": a * 2 + other}
    y_peer = {"groups": 1 - g}
    core_peer = {"heads": 1 - h}
    z_row = [lax.rem(a + d, 4) for d in range(4)]
    z_from = [lax.rem(a + 4 - d, 4) for d in range(4)]
    z_peer = [{"space": z_row[d] * 2 + b} for d in range(4)]
    kdim = kw_ref.shape[0]
    text = tsum.shape[0]
    piece = text // 4
    text_at = 6 * rows

    fetch = pltpu.make_async_copy(
        prompt_ref.at[:, pl.ds(mult(s * kdim, 128), kdim)], tcols, local_sem.at[0]
    )
    fetch.start()

    barrier = pltpu.get_barrier_semaphore()
    peers = [x_peer, y_peer, core_peer, z_peer[1], z_peer[2], z_peer[3]]
    for peer in peers:
        pl.semaphore_signal(barrier, inc=1, device_id=peer, device_id_type=MESH)

    started = []

    def send(source, target, peer):
        index = len(started)
        copy = pltpu.make_async_remote_copy(
            src_ref=source,
            dst_ref=target,
            send_sem=send_sem.at[index],
            recv_sem=recv_sem.at[index],
            device_id=peer,
            device_id_type=MESH,
        )
        copy.start()
        started.append(copy)
        return copy

    def turned(column):
        x = qkv_ref[:, pl.ds(mult(column, 128), HD)].astype(jnp.float32)
        lane = lax.broadcasted_iota(jnp.int32, x.shape, 1)
        swapped = jnp.where(lane % 2 == 0, pltpu.roll(x, HD - 1, 1), pltpu.roll(x, 1, 1))
        return (x * rope_ref[0] + swapped * rope_ref[1]).astype(jnp.bfloat16)

    def seg(row, tile):
        return pl.ds(mult((row * 2 + tile) * rows, 16), rows)

    for m in range(half):
        place = slice(m * HD, (m + 1) * HD)
        xs_kv[:, place] = turned(full + other * width + m * HD)
        xs_q[:, place] = turned(other * width + m * HD)
        kv[seg(0, b), place] = turned(full + b * width + m * HD)
    xs_kv[:, width:] = qkv_ref[:, pl.ds(mult(2 * full + other * width, 128), width)]
    kv[seg(0, b), width:] = qkv_ref[:, pl.ds(mult(2 * full + b * width, 128), width)]

    pl.semaphore_wait(barrier, len(peers))

    def text_part(which):
        cols = pl.ds(mult(which * width, 128), width)
        return [
            jnp.dot(tcols[...], w[:, cols], preferred_element_type=jnp.float32)
            for w in (kw_ref, vw_ref)
        ]

    x_kv = send(xs_kv, kv.at[seg(0, b)], x_peer)
    z_kv = [
        send(kv.at[seg(0, b)], kv.at[seg(1, b)], z_peer[1]),
        send(kv.at[seg(0, b)], kv.at[seg(2, b)], z_peer[3]),
    ]
    fetch.wait()
    key_part, value_part = text_part(other)
    txs[:, :width] = key_part.astype(jnp.bfloat16)
    txs[:, width:] = value_part.astype(jnp.bfloat16)
    x_text = send(txs, txr, x_peer)
    x_q = send(xs_q, qbuf.at[b], x_peer)

    mine = pl.ds(mult(g * width, 16), width)
    z_w = [send(ow_ref.at[mine], wbuf.at[s, mine], z_peer[d]) for d in (1, 2, 3)]
    x_w = [send(ow_ref.at[mine], wbuf.at[s, mine], x_peer)]

    key_part, value_part = text_part(b)
    tsum[:, :width] = key_part
    tsum[:, width:] = value_part
    for m in range(half):
        qbuf[b, :, m * HD : (m + 1) * HD] = turned(b * width + m * HD)
    wbuf[s] = ow_ref[...]

    x_kv.wait_recv()
    z_kv += [
        send(kv.at[seg(0, other)], kv.at[seg(1, other)], z_peer[1]),
        send(kv.at[seg(0, other)], kv.at[seg(2, other)], z_peer[3]),
    ]

    x_text.wait_recv()
    z_text = []
    for d in (1, 2, 3):
        block = pl.ds(mult(z_row[d] * piece, 16), piece)
        rss[d - 1] = (tsum[block, :] + txr[block, :].astype(jnp.float32)).astype(jnp.bfloat16)
        z_text.append(send(rss.at[d - 1], rsr.at[d - 1], z_peer[d]))
    block = pl.ds(mult(a * piece, 16), piece)
    total = tsum[block, :] + txr[block, :].astype(jnp.float32)
    for d in (1, 2, 3):
        z_text[d - 1].wait_recv()
        total = total + rsr[d - 1].astype(jnp.float32)
    own_text = pl.ds(mult(text_at + a * piece, 16), piece)
    for m in range(half):
        x = total[:, m * HD : (m + 1) * HD]
        x = x * lax.rsqrt(jnp.mean(x * x, axis=-1, keepdims=True) + eps_norm)
        kv[own_text, m * HD : (m + 1) * HD] = x.astype(jnp.bfloat16)
    kv[own_text, width:] = total[:, width:].astype(jnp.bfloat16)
    z_text_kv = [send(kv.at[own_text], kv.at[own_text], z_peer[d]) for d in (1, 2, 3)]

    y_w = []
    for d in (1, 2, 3):
        z_w[d - 1].wait_recv()
        chunk = wbuf.at[z_from[d] * 2 + b, mine]
        x_w.append(send(chunk, chunk, x_peer))
        y_w.append(send(chunk, chunk, y_peer))
    for d in range(4):
        x_w[d].wait_recv()
        chunk = wbuf.at[z_from[d] * 2 + other, mine]
        y_w.append(send(chunk, chunk, y_peer))

    for copy in [x_q] + z_kv + z_text_kv:
        copy.wait_recv()

    bias = bias_ref[...]
    for tile in (other, b):
        for m in range(half):
            place = slice(m * HD, (m + 1) * HD)
            scores = lax.dot_general(
                qbuf[tile, :, place],
                kv[:, place],
                (((1,), (1,)), ((), ())),
                preferred_element_type=jnp.float32,
            )
            scores = scores * HD ** (-0.5) + bias
            top = jnp.max(scores, axis=-1, keepdims=True)
            grown = jnp.exp(scores - top)
            scaled = grown * (1.0 / jnp.sum(grown, axis=-1, keepdims=True))
            result = jnp.dot(
                scaled.astype(jnp.bfloat16),
                kv[:, width + m * HD : width + (m + 1) * HD],
                preferred_element_type=jnp.float32,
            ).astype(jnp.bfloat16)
            if tile is other:
                att_s[:, place] = result
            else:
                att[:, pl.ds(mult(b * width + m * HD, 128), HD)] = result
        if tile is other:
            x_att = send(att_s, att.at[:, pl.ds(mult(b * width, 128), width)], x_peer)

    for copy in y_w:
        copy.wait_recv()
    x_att.wait_recv()
    cols = wbuf.shape[2]
    for j in range(4):
        part_s[:, j * cols : (j + 1) * cols] = jnp.dot(
            att[...], wbuf[(1 - h) * 4 + j], preferred_element_type=jnp.float32
        ).astype(jnp.bfloat16)
    core = send(part_s, part_r, core_peer)
    for j in range(4):
        out_ref[:, j * cols : (j + 1) * cols] = jnp.dot(
            att[...], wbuf[h * 4 + j], preferred_element_type=jnp.float32
        ).astype(jnp.bfloat16)
    core.wait_recv()
    out_ref[...] = (
        out_ref[...].astype(jnp.float32) + part_r[...].astype(jnp.float32)
    ).astype(jnp.bfloat16)
    for copy in started:
        copy.wait_send()


def rope_frequencies():
    pair = np.arange(HD) // 2
    time = np.where(pair < RT // 2, rope_theta ** (-2.0 * pair / RT), 0.0)
    first = RT // 2
    second = first + RH // 2
    height = np.where(
        (pair >= first) & (pair < second), rope_theta ** (-2.0 * (pair - first) / RH), 0.0
    )
    width = np.where(pair >= second, rope_theta ** (-2.0 * (pair - second) / RH), 0.0)
    return [value.astype(np.float32)[None, :] for value in (time, height, width)]


def fused_body(
    queries, latent_keys, latent_values, prompt, key_weight, value_weight, out_weight, tile_owner
):
    device = lax.axis_index("space")
    grid_h, grid_w = 4, 2
    tok_rows = queries.shape[0]
    full = queries.shape[1]
    head_count = full // HD
    width = full // 2
    text = prompt.shape[0]
    rows = -(-tok_rows // 16) * 16
    tile_index = jnp.arange(tile_owner.shape[0], dtype=jnp.int32)
    own_tile = jnp.sum(jnp.where(tile_owner == device, tile_index, 0))
    tile_row = own_tile // grid_w
    tile_col = own_tile % grid_w
    row_sign = jnp.where(
        (tile_owner[grid_w] // grid_w - tile_owner[0] // grid_w) % grid_h == 1, 1, -1
    )
    cell = jnp.arange(rows, dtype=jnp.int32)
    frame_pos = (cell // (TILE * TILE)).astype(jnp.float32)[:, None]
    height_pos = (tile_row * TILE + cell // TILE % TILE).astype(jnp.float32)[:, None]
    width_pos = (tile_col * TILE + cell % TILE).astype(jnp.float32)[:, None]
    time_freq, height_freq, width_freq = rope_frequencies()
    angles = frame_pos * time_freq + height_pos * height_freq + width_pos * width_freq
    sign = np.where(np.arange(HD) % 2 == 0, -1.0, 1.0).astype(np.float32)[None, :]
    rope = jnp.stack([jnp.cos(angles), jnp.sin(angles) * sign])
    step = np.repeat(np.array([0, -1, 1]), 2 * rows)
    real = np.tile(np.arange(rows) < tok_rows, 6)
    near = tile_row + row_sign * step
    latent_bias = jnp.where((near >= 0) & (near < grid_h) & real, 0.0, masked_score)
    bias = jnp.concatenate([latent_bias, jnp.zeros((text,))]).astype(jnp.float32)[None, :]
    qkv = jnp.pad(
        jnp.concatenate([queries, latent_keys, latent_values], axis=1),
        ((0, rows - tok_rows), (0, 0)),
    )
    keys = 6 * rows + text
    chunk = out_weight.shape
    bf16 = jnp.bfloat16
    vmem = pl.BlockSpec(memory_space=pltpu.VMEM)
    copies = 32
    result = pl.pallas_call(
        functools.partial(fused_kernel, rows, head_count),
        out_shape=jax.ShapeDtypeStruct((rows, 4 * chunk[1]), bf16),
        in_specs=[vmem, vmem, vmem, pl.BlockSpec(memory_space=pl.ANY), vmem, vmem, vmem],
        out_specs=vmem,
        scratch_shapes=[
            pltpu.VMEM((text, key_weight.shape[0]), bf16),
            pltpu.VMEM((rows, width), bf16),
            pltpu.VMEM((rows, full), bf16),
            pltpu.VMEM((2, rows, width), bf16),
            pltpu.VMEM((keys, full), bf16),
            pltpu.VMEM((text, full), bf16),
            pltpu.VMEM((text, full), bf16),
            pltpu.VMEM((text, full), jnp.float32),
            pltpu.VMEM((3, text // 4, full), bf16),
            pltpu.VMEM((3, text // 4, full), bf16),
            pltpu.VMEM((rows, width), bf16),
            pltpu.VMEM((rows, full), bf16),
            pltpu.VMEM((8,) + chunk, bf16),
            pltpu.VMEM((rows, 4 * chunk[1]), bf16),
            pltpu.VMEM((rows, 4 * chunk[1]), bf16),
            pltpu.SemaphoreType.DMA((1,)),
            pltpu.SemaphoreType.DMA((copies,)),
            pltpu.SemaphoreType.DMA((copies,)),
        ],
        compiler_params=pltpu.CompilerParams(
            collective_id=0, has_side_effects=True, vmem_limit_bytes=48 * 1024 * 1024
        ),
    )(rope, bias, qkv, prompt, key_weight, value_weight, out_weight)
    return result[:tok_rows]


def solution(mesh):
    in_specs = (
        P(("groups", "space"), "heads"),
        P(("groups", "space"), "heads"),
        P(("groups", "space"), "heads"),
        P("groups", None),
        P("space", "heads"),
        P("space", "heads"),
        P("heads", "space"),
        P("groups"),
    )
    out_specs = P(("groups", "space"), "heads")
    small = mesh.shape["space"] == 8 and mesh.shape["groups"] == 2 and mesh.shape["heads"] == 2
    chosen = fused_body if small else body
    return jax.shard_map(chosen, mesh=mesh, in_specs=in_specs, out_specs=out_specs, check_vma=False)
```

```python
import functools

import jax
import jax.numpy as jnp
import numpy as np
from jax import lax
from jax.experimental import pallas as pl
from jax.experimental.pallas import tpu as pltpu
from jax.sharding import PartitionSpec as P

HD = 128
RT = 16
RH = 56
TILE = 5


rope_theta = 256.0
eps_norm = 1e-06
masked_score = -1e30


def shifted(value, axis, steps):
    count = lax.axis_size(axis)
    pairs = [(source, (source + steps) % count) for source in range(count)]
    return lax.ppermute(value, axis, pairs)


def rope_tables(frame_pos, height_pos, width_pos):
    pairs_time = jnp.arange(RT // 2, dtype=jnp.float32)
    pairs_space = jnp.arange(RH // 2, dtype=jnp.float32)
    freq_time = rope_theta ** (-2.0 * pairs_time / RT)
    freq_space = rope_theta ** (-2.0 * pairs_space / RH)
    angles = jnp.concatenate(
        [
            frame_pos[:, None] * freq_time[None, :],
            height_pos[:, None] * freq_space[None, :],
            width_pos[:, None] * freq_space[None, :],
        ],
        axis=1,
    )
    return (jnp.cos(angles), jnp.sin(angles))


def rotate(stacked, cosine, sine_table):
    row_count = stacked.shape[0]
    head_total = stacked.shape[1]
    paired = stacked.reshape(row_count, head_total, HD // 2, 2)
    even_part = paired[..., 0]
    odd_part = paired[..., 1]
    cos_rows = cosine[:, None, :]
    sin_rows = sine_table[:, None, :]
    turned = jnp.stack(
        [even_part * cos_rows - odd_part * sin_rows, even_part * sin_rows + odd_part * cos_rows],
        axis=-1,
    )
    return turned.reshape(row_count, head_total * HD)


def normalize_keys(summed, head_total):
    row_count = summed.shape[0]
    half_width = summed.shape[1] // 2
    key_part = summed[:, :half_width].reshape(row_count, head_total, HD)
    key_part = key_part * lax.rsqrt(
        jnp.mean(key_part * key_part, axis=-1, keepdims=True) + eps_norm
    )
    return jnp.concatenate(
        [key_part.reshape(row_count, half_width), summed[:, half_width:]], axis=1
    ).astype(jnp.bfloat16)


def body(
    queries, latent_keys, latent_values, prompt, key_weight, value_weight, out_weight, tile_owner
):
    spaces = lax.axis_size("space")
    device = lax.axis_index("space")
    grid_h = min(8, spaces // 2)
    grid_w = spaces // grid_h
    tok_rows = queries.shape[0]
    head_width = queries.shape[1]
    head_count = head_width // HD
    tile_total = tile_owner.shape[0]
    tile_index = jnp.arange(tile_total, dtype=jnp.int32)
    own_tile = jnp.sum(jnp.where(tile_owner == device, tile_index, 0))
    tile_row = own_tile // grid_w
    tile_col = own_tile % grid_w
    anchor_slot = tile_owner[0]
    right_slot = tile_owner[min(1, tile_total - 1)]
    lower_slot = tile_owner[min(grid_w, tile_total - 1)]
    col_sign = jnp.where(right_slot % grid_w - anchor_slot % grid_w == -1, -1, 1)
    row_sign = jnp.where((lower_slot // grid_w - anchor_slot // grid_w) % grid_h == 1, 1, -1)
    cell_index = jnp.arange(tok_rows, dtype=jnp.int32)
    frame_pos = (cell_index // (TILE * TILE)).astype(jnp.float32)
    height_pos = (tile_row * TILE + cell_index // TILE % TILE).astype(jnp.float32)
    width_pos = (tile_col * TILE + cell_index % TILE).astype(jnp.float32)
    cosine, sine_table = rope_tables(frame_pos, height_pos, width_pos)
    query_rot = rotate(
        queries.astype(jnp.float32).reshape(tok_rows, head_count, HD), cosine, sine_table
    ).astype(jnp.bfloat16)
    key_rot = rotate(
        latent_keys.astype(jnp.float32).reshape(tok_rows, head_count, HD), cosine, sine_table
    ).astype(jnp.bfloat16)
    width_rows = key_weight.shape[0]
    text_cols = lax.dynamic_slice_in_dim(prompt, device * width_rows, width_rows, 1)
    both_weights = jnp.concatenate([key_weight, value_weight], axis=1)
    partial_text = jnp.dot(text_cols, both_weights, preferred_element_type=jnp.float32)
    summed_text = lax.psum(partial_text, "space")
    text_kv = normalize_keys(summed_text, head_count)
    kv_own = jnp.concatenate([key_rot, latent_values], axis=1)
    blocks = []
    valid_parts = []
    for row_step in (-1, 0, 1):
        for col_step in (-1, 0, 1):
            if row_step == 0 and col_step == 0:
                fetched = kv_own
            else:
                fetched = shifted(kv_own, "space", -(row_step * grid_w + col_step))
            near_row = tile_row + row_sign * row_step
            near_col = tile_col + col_sign * col_step
            inside = (near_row >= 0) & (near_row < grid_h) & (near_col >= 0) & (near_col < grid_w)
            blocks.append(fetched)
            valid_parts.append(jnp.zeros((tok_rows,), jnp.int32) + inside.astype(jnp.int32))
    blocks.append(text_kv)
    valid_parts.append(jnp.ones((text_kv.shape[0],), jnp.int32))
    keys_all = jnp.concatenate(blocks, axis=0)
    key_valid = jnp.concatenate(valid_parts, axis=0)
    score_scale = HD ** (-0.5)
    head_outputs = []
    for head_index in range(head_count):
        head_start = head_index * HD
        query_slice = query_rot[:, head_start : head_start + HD]
        key_slice = keys_all[:, head_start : head_start + HD]
        value_slice = keys_all[:, head_width + head_start : head_width + head_start + HD]
        scores = (
            lax.dot_general(
                query_slice, key_slice, (((1,), (1,)), ((), ())), preferred_element_type=jnp.float32
            )
            * score_scale
        )
        scores = jnp.where(key_valid[None, :] > 0, scores, masked_score)
        top_score = jnp.max(scores, axis=-1, keepdims=True)
        exponent = jnp.exp(scores - top_score)
        weights = (exponent / jnp.sum(exponent, axis=-1, keepdims=True)).astype(jnp.bfloat16)
        head_outputs.append(
            jnp.dot(weights, value_slice, preferred_element_type=jnp.float32).astype(jnp.bfloat16)
        )
    attended = jnp.concatenate(head_outputs, axis=1)
    partial_out = jnp.dot(
        attended,
        lax.all_gather(out_weight, "space", axis=1, tiled=True),
        preferred_element_type=jnp.float32,
    )
    summed_out = lax.psum_scatter(
        partial_out.astype(jnp.bfloat16), "heads", scatter_dimension=1, tiled=True
    )
    return summed_out


MESH = pl.DeviceIdType.MESH


UP_AT = 28
DOWN_AT = 31
ACROSS_AT = 34


def mult(value, step):
    return pl.multiple_of(value, step)


def fused_kernel(
    rows,
    tok_rows,
    head_count,
    owner_ref,
    table_ref,
    q_ref,
    k_ref,
    v_ref,
    prompt_ref,
    kw_hbm,
    vw_hbm,
    ow_ref,
    out_ref,
    tcols,
    kw_ref,
    vw_ref,
    padded,
    xs_q,
    xs_kv,
    qbuf,
    kv,
    txs,
    txr,
    tsum,
    near_s,
    near_r,
    far_s,
    far_r,
    att,
    wbuf,
    part_s,
    part_r,
    kept,
    swap_s,
    swap_r,
    local_sem,
    send_sem,
    recv_sem,
):
    g = lax.axis_index("groups")
    s = lax.axis_index("space")
    h = lax.axis_index("heads")
    a, b = s // 2, s % 2
    other = 1 - b
    half = head_count // 2
    width = half * HD
    full = head_count * HD
    x_peer = {"space": a * 2 + other}
    y_peer = {"groups": 1 - g}
    core_peer = {"heads": 1 - h}
    z_peer = [{"space": lax.rem(a + d, 4) * 2 + b} for d in range(4)]
    kdim = kw_hbm.shape[0]
    text = tsum.shape[0]
    piece = text // 4
    text_at = 6 * rows

    fetch = pltpu.make_async_copy(
        prompt_ref.at[:, pl.ds(mult(s * kdim, 128), kdim)], tcols, local_sem.at[0]
    )
    fetches = [
        fetch,
        pltpu.make_async_copy(kw_hbm, kw_ref, local_sem.at[1]),
        pltpu.make_async_copy(vw_hbm, vw_ref, local_sem.at[2]),
    ]
    own_w = pltpu.make_async_copy(
        ow_ref.at[pl.ds(mult(b * width, 16), width)], wbuf.at[s], local_sem.at[3]
    )
    for copy in fetches + [own_w]:
        copy.start()

    barrier = pltpu.get_barrier_semaphore()
    peers = [x_peer, y_peer, core_peer, z_peer[1], z_peer[2], z_peer[3]]
    for peer in peers:
        pl.semaphore_signal(barrier, inc=1, device_id=peer, device_id_type=MESH)

    started = []

    def send(source, target, peer):
        index = len(started)
        copy = pltpu.make_async_remote_copy(
            src_ref=source,
            dst_ref=target,
            send_sem=send_sem.at[index],
            recv_sem=recv_sem.at[index],
            device_id=peer,
            device_id_type=MESH,
        )
        copy.start()
        started.append(copy)
        return copy

    for part, ref in enumerate((q_ref, k_ref, v_ref)):
        place = slice(part * full, (part + 1) * full)
        padded[rows - 16 :, place] = jnp.zeros((16, full), jnp.float32)
        padded[:tok_rows, place] = ref[...].astype(jnp.float32)

    own_tile = jnp.int32(0)
    for t in range(8):
        own_tile = own_tile + jnp.where(owner_ref[t] == s, t, 0)
    first_row, lower_row = owner_ref[0] // 2, owner_ref[2] // 2
    row_sign = jnp.where(lax.rem(lower_row - first_row + 4, 4) == 1, 1, -1)
    tile_row = own_tile // 2
    one_hot = lax.broadcasted_iota(jnp.int32, (8, HD), 0) == own_tile
    shift_cos, shift_sin = [
        jnp.sum(
            jnp.where(one_hot, table_ref[2 * rows + 8 * k : 2 * rows + 8 * k + 8], 0.0),
            axis=0,
            keepdims=True,
        )
        for k in range(2)
    ]
    base_cos, base_sin = table_ref[:rows], table_ref[rows : 2 * rows]
    even = lax.broadcasted_iota(jnp.int32, (rows, HD), 1) % 2 == 0
    cosine = base_cos * shift_cos - base_sin * shift_sin
    sine = base_sin * shift_cos + base_cos * shift_sin
    sine = jnp.where(even, -sine, sine)

    def turned(column):
        x = padded[:, pl.ds(mult(column, 128), HD)]
        swapped = jnp.where(even, pltpu.roll(x, HD - 1, 1), pltpu.roll(x, 1, 1))
        return (x * cosine + swapped * sine).astype(jnp.bfloat16)

    def seg(row, tile):
        return pl.ds(mult((row * 2 + tile) * rows, 16), rows)

    for m in range(half):
        place = slice(m * HD, (m + 1) * HD)
        xs_kv[:, place] = turned(full + other * width + m * HD)
        xs_q[:, place] = turned(other * width + m * HD)
        kv[seg(0, b), place] = turned(full + b * width + m * HD)
    xs_kv[:, width:] = padded[:, pl.ds(mult(2 * full + other * width, 128), width)].astype(jnp.bfloat16)
    kv[seg(0, b), width:] = padded[:, pl.ds(mult(2 * full + b * width, 128), width)].astype(jnp.bfloat16)

    pl.semaphore_wait(barrier, len(peers))

    def text_part(which):
        cols = pl.ds(mult(which * width, 128), width)
        return [
            jnp.dot(tcols[...], w[:, cols], preferred_element_type=jnp.float32)
            for w in (kw_ref, vw_ref)
        ]

    x_kv = send(xs_kv, kv.at[seg(0, b)], x_peer)
    z_kv = [
        send(kv.at[seg(0, b)], kv.at[seg(1, b)], z_peer[1]),
        send(kv.at[seg(0, b)], kv.at[seg(2, b)], z_peer[3]),
    ]
    for copy in fetches:
        copy.wait()
    key_part, value_part = text_part(other)
    txs[:, :width] = key_part.astype(jnp.bfloat16)
    txs[:, width:] = value_part.astype(jnp.bfloat16)
    x_text = send(txs, txr, x_peer)
    x_q = send(xs_q, qbuf.at[b], x_peer)

    x_w = send(
        ow_ref.at[pl.ds(mult(other * width, 16), width)], wbuf.at[s], x_peer
    )

    key_part, value_part = text_part(b)
    tsum[:, :width] = key_part
    tsum[:, width:] = value_part
    for m in range(half):
        qbuf[b, :, m * HD : (m + 1) * HD] = turned(b * width + m * HD)
    own_w.wait()

    x_kv.wait_recv()
    z_kv += [
        send(kv.at[seg(0, other)], kv.at[seg(1, other)], z_peer[1]),
        send(kv.at[seg(0, other)], kv.at[seg(2, other)], z_peer[3]),
    ]

    sub = width // 2
    mine = pl.ds(mult(g * sub, 16), sub)

    def row_of_chunks(row):
        return wbuf.at[pl.ds(row * 2, 2), mine]

    def copy_at(index, view, peer):
        return pltpu.make_async_remote_copy(
            src_ref=view,
            dst_ref=view,
            send_sem=send_sem.at[index],
            recv_sem=recv_sem.at[index],
            device_id=peer,
            device_id_type=MESH,
        )

    up_peer = {"space": jnp.minimum(a + 1, 3) * 2 + b}
    down_peer = {"space": jnp.maximum(a - 1, 0) * 2 + b}

    def up_copy(k):
        return copy_at(UP_AT + k, row_of_chunks(jnp.maximum(a - k, 0)), up_peer)

    def down_copy(k):
        return copy_at(DOWN_AT + k, row_of_chunks(jnp.minimum(a + k, 3)), down_peer)

    def across_copy(d):
        return copy_at(ACROSS_AT + d, row_of_chunks(lax.rem(a + d, 4)), y_peer)

    def relay(k):
        @pl.when(a >= k + 1)
        def _():
            up_copy(k).wait_recv()
            across_copy(3 - k).start()

        if k < 2:
            @pl.when((a >= k + 1) & (a < 3))
            def _():
                up_copy(k + 1).start()

        @pl.when(a <= 2 - k)
        def _():
            down_copy(k).wait_recv()
            across_copy(1 + k).start()

        if k < 2:
            @pl.when((a <= 2 - k) & (a > 0))
            def _():
                down_copy(k + 1).start()

    x_text.wait_recv()
    parity, upper = a % 2, a // 2
    pair = 2 * piece
    near_peer = {"space": (a + 1 - 2 * parity) * 2 + b}
    far_peer = {"space": lax.rem(a + 2, 4) * 2 + b}
    block = pl.ds(mult((1 - parity) * pair, 16), pair)
    near_s[...] = (tsum[block, :] + txr[block, :].astype(jnp.float32)).astype(jnp.bfloat16)
    near_text = send(near_s, near_r, near_peer)
    block = pl.ds(mult(parity * pair, 16), pair)
    tsum[block, :] = tsum[block, :] + txr[block, :].astype(jnp.float32)

    x_w.wait_recv()

    @pl.when(a < 3)
    def _():
        up_copy(0).start()

    @pl.when(a > 0)
    def _():
        down_copy(0).start()

    near_text.wait_recv()
    lower_half = pl.ds(mult((1 - upper) * piece, 16), piece)
    block = pl.ds(mult(parity * pair + (1 - upper) * piece, 16), piece)
    far_s[...] = (tsum[block, :] + near_r[lower_half, :].astype(jnp.float32)).astype(jnp.bfloat16)
    far_text = send(far_s, far_r, far_peer)
    kept_half = pl.ds(mult(upper * piece, 16), piece)
    block = pl.ds(mult(parity * pair + upper * piece, 16), piece)
    total = tsum[block, :] + near_r[kept_half, :].astype(jnp.float32)
    far_text.wait_recv()
    total = total + far_r[...].astype(jnp.float32)
    own_text = pl.ds(mult(text_at + parity * pair + upper * piece, 16), piece)
    far_rows = pl.ds(mult(text_at + parity * pair + (1 - upper) * piece, 16), piece)
    for m in range(half):
        x = total[:, m * HD : (m + 1) * HD]
        x = x * lax.rsqrt(jnp.mean(x * x, axis=-1, keepdims=True) + eps_norm)
        kv[own_text, m * HD : (m + 1) * HD] = x.astype(jnp.bfloat16)
    kv[own_text, width:] = total[:, width:].astype(jnp.bfloat16)
    far_kv = send(kv.at[own_text], kv.at[own_text], far_peer)
    near_kv = send(kv.at[own_text], kv.at[own_text], near_peer)
    far_kv.wait_recv()
    near_kv2 = send(kv.at[far_rows], kv.at[far_rows], near_peer)

    relay(0)
    z_text_kv = [near_kv, near_kv2]
    for copy in [x_q] + z_kv + z_text_kv:
        copy.wait_recv()

    key_at = lax.broadcasted_iota(jnp.int32, (1, kv.shape[0]), 1)
    bias = jnp.where(key_at >= text_at, 0.0, masked_score)
    for row, step in enumerate((0, -1, 1)):
        near = tile_row + row_sign * step
        level = jnp.where((near >= 0) & (near < 4), 0.0, masked_score)
        for tile in range(2):
            low = (row * 2 + tile) * rows
            bias = jnp.where((key_at >= low) & (key_at < low + tok_rows), level, bias)
    for tile in (other, b):
        for m in range(half):
            place = slice(m * HD, (m + 1) * HD)
            scores = lax.dot_general(
                qbuf[tile, :, place],
                kv[:, place],
                (((1,), (1,)), ((), ())),
                preferred_element_type=jnp.float32,
            )
            scores = scores * HD ** (-0.5) + bias
            top = jnp.max(scores, axis=-1, keepdims=True)
            grown = jnp.exp(scores - top)
            scaled = grown * (1.0 / jnp.sum(grown, axis=-1, keepdims=True))
            result = jnp.dot(
                scaled.astype(jnp.bfloat16),
                kv[:, width + m * HD : width + (m + 1) * HD],
                preferred_element_type=jnp.float32,
            ).astype(jnp.bfloat16)
            att[pl.ds(mult(tile * rows, 16), rows), place] = result
        relay(1 if tile is other else 2)

    for d in (1, 2, 3):
        across_copy(d).wait_recv()
    cols = wbuf.shape[2]
    core = []
    for j in range(4):
        part_s[j] = jnp.dot(
            att[...], wbuf[(1 - h) * 4 + j], preferred_element_type=jnp.float32
        ).astype(jnp.bfloat16)
        core.append(send(part_s.at[j], part_r.at[j], core_peer))
    for j in range(4):
        kept[j] = jnp.dot(att[...], wbuf[h * 4 + j], preferred_element_type=jnp.float32)
    sent_rows = pl.ds(mult(other * rows, 16), rows)
    own_rows = pl.ds(mult(b * rows, 16), rows)
    swap = []
    for j in range(4):
        core[j].wait_recv()
        swap_s[j] = (
            kept[j, sent_rows, :] + part_r[j, sent_rows, :].astype(jnp.float32)
        ).astype(jnp.bfloat16)
        swap.append(send(swap_s.at[j], swap_r.at[j], x_peer))
    for j in range(4):
        total = kept[j, own_rows, :] + part_r[j, own_rows, :].astype(jnp.float32)
        swap[j].wait_recv()
        out_ref[:, j * cols : (j + 1) * cols] = (
            total + swap_r[j].astype(jnp.float32)
        ).astype(jnp.bfloat16)

    for copy in started:
        copy.wait_send()
    for d in (1, 2, 3):
        across_copy(d).wait_send()
    for k in range(3):
        @pl.when((a >= k) & (a < 3))
        def _():
            up_copy(k).wait_send()

        @pl.when((a <= 3 - k) & (a > 0))
        def _():
            down_copy(k).wait_send()


def rope_constants(rows):
    pair = np.arange(HD) // 2
    first = RT // 2
    second = first + RH // 2
    in_height = (pair >= first) & (pair < second)
    time = np.where(pair < first, rope_theta ** (-2.0 * pair / RT), 0.0)
    height = np.where(in_height, rope_theta ** (-2.0 * (pair - first) / RH), 0.0)
    width = np.where(pair >= second, rope_theta ** (-2.0 * (pair - second) / RH), 0.0)
    cell = np.arange(rows)[:, None]
    base = cell // (TILE * TILE) * time + cell // TILE % TILE * height + cell % TILE * width
    tile = np.arange(8)[:, None]
    shift = tile // 2 * TILE * height + tile % 2 * TILE * width
    tables = [np.cos(base), np.sin(base), np.cos(shift), np.sin(shift)]
    return np.concatenate(tables).astype(np.float32)


def fused_body(
    queries, latent_keys, latent_values, prompt, key_weight, value_weight, out_weight, tile_owner
):
    tok_rows = queries.shape[0]
    full = queries.shape[1]
    head_count = full // HD
    width = full // 2
    text = prompt.shape[0]
    rows = -(-tok_rows // 16) * 16
    keys = 6 * rows + text
    chunk = out_weight.shape
    bf16 = jnp.bfloat16
    vmem = pl.BlockSpec(memory_space=pltpu.VMEM)
    smem = pl.BlockSpec(memory_space=pltpu.SMEM)
    hbm = pl.BlockSpec(memory_space=pltpu.HBM)
    copies = 40
    result = pl.pallas_call(
        functools.partial(fused_kernel, rows, tok_rows, head_count),
        out_shape=jax.ShapeDtypeStruct((rows, 4 * chunk[1]), bf16),
        in_specs=[smem, vmem, vmem, vmem, vmem, hbm, hbm, hbm, hbm],
        out_specs=vmem,
        scratch_shapes=[
            pltpu.VMEM((text, key_weight.shape[0]), bf16),
            pltpu.VMEM(key_weight.shape, bf16),
            pltpu.VMEM(key_weight.shape, bf16),
            pltpu.VMEM((rows, 3 * full), jnp.float32),
            pltpu.VMEM((rows, width), bf16),
            pltpu.VMEM((rows, full), bf16),
            pltpu.VMEM((2, rows, width), bf16),
            pltpu.VMEM((keys, full), bf16),
            pltpu.VMEM((text, full), bf16),
            pltpu.VMEM((text, full), bf16),
            pltpu.VMEM((text, full), jnp.float32),
            pltpu.VMEM((text // 2, full), bf16),
            pltpu.VMEM((text // 2, full), bf16),
            pltpu.VMEM((text // 4, full), bf16),
            pltpu.VMEM((text // 4, full), bf16),
            pltpu.VMEM((2 * rows, width), bf16),
            pltpu.VMEM((8, width, chunk[1]), bf16),
            pltpu.VMEM((4, 2 * rows, chunk[1]), bf16),
            pltpu.VMEM((4, 2 * rows, chunk[1]), bf16),
            pltpu.VMEM((4, 2 * rows, chunk[1]), jnp.float32),
            pltpu.VMEM((4, rows, chunk[1]), bf16),
            pltpu.VMEM((4, rows, chunk[1]), bf16),
            pltpu.SemaphoreType.DMA((4,)),
            pltpu.SemaphoreType.DMA((copies,)),
            pltpu.SemaphoreType.DMA((copies,)),
        ],
        compiler_params=pltpu.CompilerParams(
            collective_id=0, has_side_effects=True, vmem_limit_bytes=60 * 1024 * 1024
        ),
    )(
        tile_owner,
        rope_constants(rows),
        queries,
        latent_keys,
        latent_values,
        prompt,
        key_weight,
        value_weight,
        out_weight,
    )
    return result[:tok_rows]


def solution(mesh):
    in_specs = (
        P(("groups", "space"), "heads"),
        P(("groups", "space"), "heads"),
        P(("groups", "space"), "heads"),
        P("groups", None),
        P("space", "heads"),
        P("space", "heads"),
        P("heads", "space"),
        P("groups"),
    )
    out_specs = P(("groups", "space"), "heads")
    small = mesh.shape["space"] == 8 and mesh.shape["groups"] == 2 and mesh.shape["heads"] == 2
    chosen = fused_body if small else body
    return jax.shard_map(chosen, mesh=mesh, in_specs=in_specs, out_specs=out_specs, check_vma=False)
```

```python
import functools

import jax
import jax.numpy as jnp
import numpy as np
from jax import lax
from jax.experimental import pallas as pl
from jax.experimental.pallas import tpu as pltpu
from jax.sharding import PartitionSpec as P

HD = 128
RT = 16
RH = 56
TILE = 5


rope_theta = 256.0
eps_norm = 1e-06
masked_score = -1e30


def shifted(value, axis, steps):
    count = lax.axis_size(axis)
    pairs = [(source, (source + steps) % count) for source in range(count)]
    return lax.ppermute(value, axis, pairs)


def rope_tables(frame_pos, height_pos, width_pos):
    pairs_time = jnp.arange(RT // 2, dtype=jnp.float32)
    pairs_space = jnp.arange(RH // 2, dtype=jnp.float32)
    freq_time = rope_theta ** (-2.0 * pairs_time / RT)
    freq_space = rope_theta ** (-2.0 * pairs_space / RH)
    angles = jnp.concatenate(
        [
            frame_pos[:, None] * freq_time[None, :],
            height_pos[:, None] * freq_space[None, :],
            width_pos[:, None] * freq_space[None, :],
        ],
        axis=1,
    )
    return (jnp.cos(angles), jnp.sin(angles))


def rotate(stacked, cosine, sine_table):
    row_count = stacked.shape[0]
    head_total = stacked.shape[1]
    paired = stacked.reshape(row_count, head_total, HD // 2, 2)
    even_part = paired[..., 0]
    odd_part = paired[..., 1]
    cos_rows = cosine[:, None, :]
    sin_rows = sine_table[:, None, :]
    turned = jnp.stack(
        [even_part * cos_rows - odd_part * sin_rows, even_part * sin_rows + odd_part * cos_rows],
        axis=-1,
    )
    return turned.reshape(row_count, head_total * HD)


def normalize_keys(summed, head_total):
    row_count = summed.shape[0]
    half_width = summed.shape[1] // 2
    key_part = summed[:, :half_width].reshape(row_count, head_total, HD)
    key_part = key_part * lax.rsqrt(
        jnp.mean(key_part * key_part, axis=-1, keepdims=True) + eps_norm
    )
    return jnp.concatenate(
        [key_part.reshape(row_count, half_width), summed[:, half_width:]], axis=1
    ).astype(jnp.bfloat16)


def body(
    queries, latent_keys, latent_values, prompt, key_weight, value_weight, out_weight, tile_owner
):
    spaces = lax.axis_size("space")
    device = lax.axis_index("space")
    grid_h = min(8, spaces // 2)
    grid_w = spaces // grid_h
    tok_rows = queries.shape[0]
    head_width = queries.shape[1]
    head_count = head_width // HD
    tile_total = tile_owner.shape[0]
    tile_index = jnp.arange(tile_total, dtype=jnp.int32)
    own_tile = jnp.sum(jnp.where(tile_owner == device, tile_index, 0))
    tile_row = own_tile // grid_w
    tile_col = own_tile % grid_w
    anchor_slot = tile_owner[0]
    right_slot = tile_owner[min(1, tile_total - 1)]
    lower_slot = tile_owner[min(grid_w, tile_total - 1)]
    col_sign = jnp.where(right_slot % grid_w - anchor_slot % grid_w == -1, -1, 1)
    row_sign = jnp.where((lower_slot // grid_w - anchor_slot // grid_w) % grid_h == 1, 1, -1)
    cell_index = jnp.arange(tok_rows, dtype=jnp.int32)
    frame_pos = (cell_index // (TILE * TILE)).astype(jnp.float32)
    height_pos = (tile_row * TILE + cell_index // TILE % TILE).astype(jnp.float32)
    width_pos = (tile_col * TILE + cell_index % TILE).astype(jnp.float32)
    cosine, sine_table = rope_tables(frame_pos, height_pos, width_pos)
    query_rot = rotate(
        queries.astype(jnp.float32).reshape(tok_rows, head_count, HD), cosine, sine_table
    ).astype(jnp.bfloat16)
    key_rot = rotate(
        latent_keys.astype(jnp.float32).reshape(tok_rows, head_count, HD), cosine, sine_table
    ).astype(jnp.bfloat16)
    width_rows = key_weight.shape[0]
    text_cols = lax.dynamic_slice_in_dim(prompt, device * width_rows, width_rows, 1)
    both_weights = jnp.concatenate([key_weight, value_weight], axis=1)
    partial_text = jnp.dot(text_cols, both_weights, preferred_element_type=jnp.float32)
    summed_text = lax.psum(partial_text, "space")
    text_kv = normalize_keys(summed_text, head_count)
    kv_own = jnp.concatenate([key_rot, latent_values], axis=1)
    blocks = []
    valid_parts = []
    for row_step in (-1, 0, 1):
        for col_step in (-1, 0, 1):
            if row_step == 0 and col_step == 0:
                fetched = kv_own
            else:
                fetched = shifted(kv_own, "space", -(row_step * grid_w + col_step))
            near_row = tile_row + row_sign * row_step
            near_col = tile_col + col_sign * col_step
            inside = (near_row >= 0) & (near_row < grid_h) & (near_col >= 0) & (near_col < grid_w)
            blocks.append(fetched)
            valid_parts.append(jnp.zeros((tok_rows,), jnp.int32) + inside.astype(jnp.int32))
    blocks.append(text_kv)
    valid_parts.append(jnp.ones((text_kv.shape[0],), jnp.int32))
    keys_all = jnp.concatenate(blocks, axis=0)
    key_valid = jnp.concatenate(valid_parts, axis=0)
    score_scale = HD ** (-0.5)
    head_outputs = []
    for head_index in range(head_count):
        head_start = head_index * HD
        query_slice = query_rot[:, head_start : head_start + HD]
        key_slice = keys_all[:, head_start : head_start + HD]
        value_slice = keys_all[:, head_width + head_start : head_width + head_start + HD]
        scores = (
            lax.dot_general(
                query_slice, key_slice, (((1,), (1,)), ((), ())), preferred_element_type=jnp.float32
            )
            * score_scale
        )
        scores = jnp.where(key_valid[None, :] > 0, scores, masked_score)
        top_score = jnp.max(scores, axis=-1, keepdims=True)
        exponent = jnp.exp(scores - top_score)
        weights = (exponent / jnp.sum(exponent, axis=-1, keepdims=True)).astype(jnp.bfloat16)
        head_outputs.append(
            jnp.dot(weights, value_slice, preferred_element_type=jnp.float32).astype(jnp.bfloat16)
        )
    attended = jnp.concatenate(head_outputs, axis=1)
    partial_out = jnp.dot(
        attended,
        lax.all_gather(out_weight, "space", axis=1, tiled=True),
        preferred_element_type=jnp.float32,
    )
    summed_out = lax.psum_scatter(
        partial_out.astype(jnp.bfloat16), "heads", scatter_dimension=1, tiled=True
    )
    return summed_out


MESH = pl.DeviceIdType.MESH


UP_AT = 28
DOWN_AT = 31
ACROSS_AT = 34


def mult(value, step):
    return pl.multiple_of(value, step)


def fused_kernel(
    rows,
    tok_rows,
    head_count,
    owner_ref,
    table_ref,
    q_ref,
    k_ref,
    v_ref,
    prompt_ref,
    kw_hbm,
    vw_hbm,
    ow_ref,
    out_ref,
    tcols,
    kw_ref,
    vw_ref,
    padded,
    xs_q,
    xs_kv,
    qbuf,
    kv,
    txs,
    txr,
    tsum,
    near_s,
    near_r,
    far_s,
    far_r,
    att,
    wbuf,
    part_s,
    part_r,
    kept,
    swap_s,
    swap_r,
    local_sem,
    send_sem,
    recv_sem,
):
    g = lax.axis_index("groups")
    s = lax.axis_index("space")
    h = lax.axis_index("heads")
    a, b = s // 2, s % 2
    other = 1 - b
    half = head_count // 2
    width = half * HD
    full = head_count * HD
    x_peer = {"space": a * 2 + other}
    y_peer = {"groups": 1 - g}
    core_peer = {"heads": 1 - h}
    z_peer = [{"space": lax.rem(a + d, 4) * 2 + b} for d in range(4)]
    kdim = kw_hbm.shape[0]
    text = tsum.shape[0]
    piece = text // 4
    text_at = 6 * rows

    fetch = pltpu.make_async_copy(
        prompt_ref.at[:, pl.ds(mult(s * kdim, 128), kdim)], tcols, local_sem.at[0]
    )
    fetches = [
        fetch,
        pltpu.make_async_copy(kw_hbm, kw_ref, local_sem.at[1]),
        pltpu.make_async_copy(vw_hbm, vw_ref, local_sem.at[2]),
    ]
    own_w = pltpu.make_async_copy(
        ow_ref.at[pl.ds(mult(b * width, 16), width)], wbuf.at[s], local_sem.at[3]
    )
    for copy in fetches + [own_w]:
        copy.start()

    barrier = pltpu.get_barrier_semaphore()
    peers = [x_peer, y_peer, core_peer, z_peer[1], z_peer[2], z_peer[3]]
    for peer in peers:
        pl.semaphore_signal(barrier, inc=1, device_id=peer, device_id_type=MESH)

    started = []

    def send(source, target, peer):
        index = len(started)
        copy = pltpu.make_async_remote_copy(
            src_ref=source,
            dst_ref=target,
            send_sem=send_sem.at[index],
            recv_sem=recv_sem.at[index],
            device_id=peer,
            device_id_type=MESH,
        )
        copy.start()
        started.append(copy)
        return copy

    def text_part(which):
        cols = pl.ds(mult(which * width, 128), width)
        return [
            jnp.dot(tcols[...], w[:, cols], preferred_element_type=jnp.float32)
            for w in (kw_ref, vw_ref)
        ]

    for copy in fetches:
        copy.wait()
    key_part, value_part = text_part(other)
    txs[:, :width] = key_part.astype(jnp.bfloat16)
    txs[:, width:] = value_part.astype(jnp.bfloat16)
    pl.semaphore_wait(barrier, len(peers))

    x_text = send(txs, txr, x_peer)

    x_w = send(
        ow_ref.at[pl.ds(mult(other * width, 16), width)], wbuf.at[s], x_peer
    )

    for part, ref in enumerate((q_ref, k_ref, v_ref)):
        place = slice(part * full, (part + 1) * full)
        padded[rows - 16 :, place] = jnp.zeros((16, full), jnp.float32)
        padded[:tok_rows, place] = ref[...].astype(jnp.float32)

    own_tile = jnp.int32(0)
    for t in range(8):
        own_tile = own_tile + jnp.where(owner_ref[t] == s, t, 0)
    first_row, lower_row = owner_ref[0] // 2, owner_ref[2] // 2
    row_sign = jnp.where(lax.rem(lower_row - first_row + 4, 4) == 1, 1, -1)
    tile_row = own_tile // 2
    one_hot = lax.broadcasted_iota(jnp.int32, (8, HD), 0) == own_tile
    shift_cos, shift_sin = [
        jnp.sum(
            jnp.where(one_hot, table_ref[2 * rows + 8 * k : 2 * rows + 8 * k + 8], 0.0),
            axis=0,
            keepdims=True,
        )
        for k in range(2)
    ]
    base_cos, base_sin = table_ref[:rows], table_ref[rows : 2 * rows]
    even = lax.broadcasted_iota(jnp.int32, (rows, HD), 1) % 2 == 0
    cosine = base_cos * shift_cos - base_sin * shift_sin
    sine = base_sin * shift_cos + base_cos * shift_sin
    sine = jnp.where(even, -sine, sine)

    def turned(column):
        x = padded[:, pl.ds(mult(column, 128), HD)]
        swapped = jnp.where(even, pltpu.roll(x, HD - 1, 1), pltpu.roll(x, 1, 1))
        return (x * cosine + swapped * sine).astype(jnp.bfloat16)

    def seg(row, tile):
        return pl.ds(mult((row * 2 + tile) * rows, 16), rows)

    for m in range(half):
        place = slice(m * HD, (m + 1) * HD)
        xs_kv[:, place] = turned(full + other * width + m * HD)
        xs_q[:, place] = turned(other * width + m * HD)
        kv[seg(0, b), place] = turned(full + b * width + m * HD)
    xs_kv[:, width:] = padded[:, pl.ds(mult(2 * full + other * width, 128), width)].astype(jnp.bfloat16)
    kv[seg(0, b), width:] = padded[:, pl.ds(mult(2 * full + b * width, 128), width)].astype(jnp.bfloat16)

    x_kv = send(xs_kv, kv.at[seg(0, b)], x_peer)
    z_kv = [
        send(kv.at[seg(0, b)], kv.at[seg(1, b)], z_peer[1]),
        send(kv.at[seg(0, b)], kv.at[seg(2, b)], z_peer[3]),
    ]
    x_q = send(xs_q, qbuf.at[b], x_peer)

    key_part, value_part = text_part(b)
    tsum[:, :width] = key_part
    tsum[:, width:] = value_part
    for m in range(half):
        qbuf[b, :, m * HD : (m + 1) * HD] = turned(b * width + m * HD)
    own_w.wait()

    x_kv.wait_recv()
    z_kv += [
        send(kv.at[seg(0, other)], kv.at[seg(1, other)], z_peer[1]),
        send(kv.at[seg(0, other)], kv.at[seg(2, other)], z_peer[3]),
    ]

    sub = width // 2
    mine = pl.ds(mult(g * sub, 16), sub)

    def row_of_chunks(row):
        return wbuf.at[pl.ds(row * 2, 2), mine]

    def copy_at(index, view, peer):
        return pltpu.make_async_remote_copy(
            src_ref=view,
            dst_ref=view,
            send_sem=send_sem.at[index],
            recv_sem=recv_sem.at[index],
            device_id=peer,
            device_id_type=MESH,
        )

    up_peer = {"space": jnp.minimum(a + 1, 3) * 2 + b}
    down_peer = {"space": jnp.maximum(a - 1, 0) * 2 + b}

    def up_copy(k):
        return copy_at(UP_AT + k, row_of_chunks(jnp.maximum(a - k, 0)), up_peer)

    def down_copy(k):
        return copy_at(DOWN_AT + k, row_of_chunks(jnp.minimum(a + k, 3)), down_peer)

    def across_copy(d):
        return copy_at(ACROSS_AT + d, row_of_chunks(lax.rem(a + d, 4)), y_peer)

    def relay(k):
        @pl.when(a >= k + 1)
        def _():
            up_copy(k).wait_recv()
            across_copy(3 - k).start()

        if k < 2:
            @pl.when((a >= k + 1) & (a < 3))
            def _():
                up_copy(k + 1).start()

        @pl.when(a <= 2 - k)
        def _():
            down_copy(k).wait_recv()
            across_copy(1 + k).start()

        if k < 2:
            @pl.when((a <= 2 - k) & (a > 0))
            def _():
                down_copy(k + 1).start()

    x_text.wait_recv()
    parity, upper = a % 2, a // 2
    pair = 2 * piece
    near_peer = {"space": (a + 1 - 2 * parity) * 2 + b}
    far_peer = {"space": lax.rem(a + 2, 4) * 2 + b}
    block = pl.ds(mult((1 - parity) * pair, 16), pair)
    near_s[...] = (tsum[block, :] + txr[block, :].astype(jnp.float32)).astype(jnp.bfloat16)
    near_text = send(near_s, near_r, near_peer)
    block = pl.ds(mult(parity * pair, 16), pair)
    tsum[block, :] = tsum[block, :] + txr[block, :].astype(jnp.float32)

    x_w.wait_recv()

    @pl.when(a < 3)
    def _():
        up_copy(0).start()

    @pl.when(a > 0)
    def _():
        down_copy(0).start()

    near_text.wait_recv()
    lower_half = pl.ds(mult((1 - upper) * piece, 16), piece)
    block = pl.ds(mult(parity * pair + (1 - upper) * piece, 16), piece)
    far_s[...] = (tsum[block, :] + near_r[lower_half, :].astype(jnp.float32)).astype(jnp.bfloat16)
    far_text = send(far_s, far_r, far_peer)
    kept_half = pl.ds(mult(upper * piece, 16), piece)
    block = pl.ds(mult(parity * pair + upper * piece, 16), piece)
    total = tsum[block, :] + near_r[kept_half, :].astype(jnp.float32)
    far_text.wait_recv()
    total = total + far_r[...].astype(jnp.float32)
    own_text = pl.ds(mult(text_at + parity * pair + upper * piece, 16), piece)
    far_rows = pl.ds(mult(text_at + parity * pair + (1 - upper) * piece, 16), piece)
    for m in range(half):
        x = total[:, m * HD : (m + 1) * HD]
        x = x * lax.rsqrt(jnp.mean(x * x, axis=-1, keepdims=True) + eps_norm)
        kv[own_text, m * HD : (m + 1) * HD] = x.astype(jnp.bfloat16)
    kv[own_text, width:] = total[:, width:].astype(jnp.bfloat16)
    far_kv = send(kv.at[own_text], kv.at[own_text], far_peer)
    near_kv = send(kv.at[own_text], kv.at[own_text], near_peer)
    relay(0)
    far_kv.wait_recv()
    near_kv2 = send(kv.at[far_rows], kv.at[far_rows], near_peer)

    relay(1)
    z_text_kv = [near_kv, near_kv2]
    for copy in [x_q] + z_kv + z_text_kv:
        copy.wait_recv()

    key_at = lax.broadcasted_iota(jnp.int32, (1, kv.shape[0]), 1)
    bias = jnp.where(key_at >= text_at, 0.0, masked_score)
    for row, step in enumerate((0, -1, 1)):
        near = tile_row + row_sign * step
        level = jnp.where((near >= 0) & (near < 4), 0.0, masked_score)
        for tile in range(2):
            low = (row * 2 + tile) * rows
            bias = jnp.where((key_at >= low) & (key_at < low + tok_rows), level, bias)
    for tile in (other, b):
        for m in range(half):
            place = slice(m * HD, (m + 1) * HD)
            scores = lax.dot_general(
                qbuf[tile, :, place],
                kv[:, place],
                (((1,), (1,)), ((), ())),
                preferred_element_type=jnp.float32,
            )
            scores = scores * HD ** (-0.5) + bias
            top = jnp.max(scores, axis=-1, keepdims=True)
            grown = jnp.exp(scores - top)
            scaled = grown * (1.0 / jnp.sum(grown, axis=-1, keepdims=True))
            result = jnp.dot(
                scaled.astype(jnp.bfloat16),
                kv[:, width + m * HD : width + (m + 1) * HD],
                preferred_element_type=jnp.float32,
            ).astype(jnp.bfloat16)
            att[pl.ds(mult(tile * rows, 16), rows), place] = result
        if tile is other:
            relay(2)

    for d in (1, 2, 3):
        across_copy(d).wait_recv()
    cols = wbuf.shape[2]
    core = []
    for j in range(4):
        part_s[j] = jnp.dot(
            att[...], wbuf[(1 - h) * 4 + j], preferred_element_type=jnp.float32
        ).astype(jnp.bfloat16)
        core.append(send(part_s.at[j], part_r.at[j], core_peer))
    for j in range(4):
        kept[j] = jnp.dot(att[...], wbuf[h * 4 + j], preferred_element_type=jnp.float32)
    sent_rows = pl.ds(mult(other * rows, 16), rows)
    own_rows = pl.ds(mult(b * rows, 16), rows)
    swap = []
    for j in range(4):
        core[j].wait_recv()
        swap_s[j] = (
            kept[j, sent_rows, :] + part_r[j, sent_rows, :].astype(jnp.float32)
        ).astype(jnp.bfloat16)
        swap.append(send(swap_s.at[j], swap_r.at[j], x_peer))
    for j in range(4):
        total = kept[j, own_rows, :] + part_r[j, own_rows, :].astype(jnp.float32)
        swap[j].wait_recv()
        out_ref[:, j * cols : (j + 1) * cols] = (
            total + swap_r[j].astype(jnp.float32)
        ).astype(jnp.bfloat16)

    for copy in started:
        copy.wait_send()
    for d in (1, 2, 3):
        across_copy(d).wait_send()
    for k in range(3):
        @pl.when((a >= k) & (a < 3))
        def _():
            up_copy(k).wait_send()

        @pl.when((a <= 3 - k) & (a > 0))
        def _():
            down_copy(k).wait_send()


def rope_constants(rows):
    pair = np.arange(HD) // 2
    first = RT // 2
    second = first + RH // 2
    in_height = (pair >= first) & (pair < second)
    time = np.where(pair < first, rope_theta ** (-2.0 * pair / RT), 0.0)
    height = np.where(in_height, rope_theta ** (-2.0 * (pair - first) / RH), 0.0)
    width = np.where(pair >= second, rope_theta ** (-2.0 * (pair - second) / RH), 0.0)
    cell = np.arange(rows)[:, None]
    base = cell // (TILE * TILE) * time + cell // TILE % TILE * height + cell % TILE * width
    tile = np.arange(8)[:, None]
    shift = tile // 2 * TILE * height + tile % 2 * TILE * width
    tables = [np.cos(base), np.sin(base), np.cos(shift), np.sin(shift)]
    return np.concatenate(tables).astype(np.float32)


def fused_body(
    queries, latent_keys, latent_values, prompt, key_weight, value_weight, out_weight, tile_owner
):
    tok_rows = queries.shape[0]
    full = queries.shape[1]
    head_count = full // HD
    width = full // 2
    text = prompt.shape[0]
    rows = -(-tok_rows // 16) * 16
    keys = 6 * rows + text
    chunk = out_weight.shape
    bf16 = jnp.bfloat16
    vmem = pl.BlockSpec(memory_space=pltpu.VMEM)
    smem = pl.BlockSpec(memory_space=pltpu.SMEM)
    hbm = pl.BlockSpec(memory_space=pltpu.HBM)
    copies = 40
    result = pl.pallas_call(
        functools.partial(fused_kernel, rows, tok_rows, head_count),
        out_shape=jax.ShapeDtypeStruct((rows, 4 * chunk[1]), bf16),
        in_specs=[smem, vmem, vmem, vmem, vmem, hbm, hbm, hbm, hbm],
        out_specs=vmem,
        scratch_shapes=[
            pltpu.VMEM((text, key_weight.shape[0]), bf16),
            pltpu.VMEM(key_weight.shape, bf16),
            pltpu.VMEM(key_weight.shape, bf16),
            pltpu.VMEM((rows, 3 * full), jnp.float32),
            pltpu.VMEM((rows, width), bf16),
            pltpu.VMEM((rows, full), bf16),
            pltpu.VMEM((2, rows, width), bf16),
            pltpu.VMEM((keys, full), bf16),
            pltpu.VMEM((text, full), bf16),
            pltpu.VMEM((text, full), bf16),
            pltpu.VMEM((text, full), jnp.float32),
            pltpu.VMEM((text // 2, full), bf16),
            pltpu.VMEM((text // 2, full), bf16),
            pltpu.VMEM((text // 4, full), bf16),
            pltpu.VMEM((text // 4, full), bf16),
            pltpu.VMEM((2 * rows, width), bf16),
            pltpu.VMEM((8, width, chunk[1]), bf16),
            pltpu.VMEM((4, 2 * rows, chunk[1]), bf16),
            pltpu.VMEM((4, 2 * rows, chunk[1]), bf16),
            pltpu.VMEM((4, 2 * rows, chunk[1]), jnp.float32),
            pltpu.VMEM((4, rows, chunk[1]), bf16),
            pltpu.VMEM((4, rows, chunk[1]), bf16),
            pltpu.SemaphoreType.DMA((4,)),
            pltpu.SemaphoreType.DMA((copies,)),
            pltpu.SemaphoreType.DMA((copies,)),
        ],
        compiler_params=pltpu.CompilerParams(
            collective_id=0, has_side_effects=True, vmem_limit_bytes=60 * 1024 * 1024
        ),
    )(
        tile_owner,
        rope_constants(rows),
        queries,
        latent_keys,
        latent_values,
        prompt,
        key_weight,
        value_weight,
        out_weight,
    )
    return result[:tok_rows]


def solution(mesh):
    in_specs = (
        P(("groups", "space"), "heads"),
        P(("groups", "space"), "heads"),
        P(("groups", "space"), "heads"),
        P("groups", None),
        P("space", "heads"),
        P("space", "heads"),
        P("heads", "space"),
        P("groups"),
    )
    out_specs = P(("groups", "space"), "heads")
    small = mesh.shape["space"] == 8 and mesh.shape["groups"] == 2 and mesh.shape["heads"] == 2
    chosen = fused_body if small else body
    return jax.shard_map(chosen, mesh=mesh, in_specs=in_specs, out_specs=out_specs, check_vma=False)
```

```python
import functools

import jax
import jax.numpy as jnp
import numpy as np
from jax import lax
from jax.experimental import pallas as pl
from jax.experimental.pallas import tpu as pltpu
from jax.sharding import PartitionSpec as P

HD = 128
RT = 16
RH = 56
TILE = 5


rope_theta = 256.0
eps_norm = 1e-06
masked_score = -1e30


def shifted(value, axis, steps):
    count = lax.axis_size(axis)
    pairs = [(source, (source + steps) % count) for source in range(count)]
    return lax.ppermute(value, axis, pairs)


def rope_tables(frame_pos, height_pos, width_pos):
    pairs_time = jnp.arange(RT // 2, dtype=jnp.float32)
    pairs_space = jnp.arange(RH // 2, dtype=jnp.float32)
    freq_time = rope_theta ** (-2.0 * pairs_time / RT)
    freq_space = rope_theta ** (-2.0 * pairs_space / RH)
    angles = jnp.concatenate(
        [
            frame_pos[:, None] * freq_time[None, :],
            height_pos[:, None] * freq_space[None, :],
            width_pos[:, None] * freq_space[None, :],
        ],
        axis=1,
    )
    return (jnp.cos(angles), jnp.sin(angles))


def rotate(stacked, cosine, sine_table):
    row_count = stacked.shape[0]
    head_total = stacked.shape[1]
    paired = stacked.reshape(row_count, head_total, HD // 2, 2)
    even_part = paired[..., 0]
    odd_part = paired[..., 1]
    cos_rows = cosine[:, None, :]
    sin_rows = sine_table[:, None, :]
    turned = jnp.stack(
        [even_part * cos_rows - odd_part * sin_rows, even_part * sin_rows + odd_part * cos_rows],
        axis=-1,
    )
    return turned.reshape(row_count, head_total * HD)


def normalize_keys(summed, head_total):
    row_count = summed.shape[0]
    half_width = summed.shape[1] // 2
    key_part = summed[:, :half_width].reshape(row_count, head_total, HD)
    key_part = key_part * lax.rsqrt(
        jnp.mean(key_part * key_part, axis=-1, keepdims=True) + eps_norm
    )
    return jnp.concatenate(
        [key_part.reshape(row_count, half_width), summed[:, half_width:]], axis=1
    ).astype(jnp.bfloat16)


def body(
    queries, latent_keys, latent_values, prompt, key_weight, value_weight, out_weight, tile_owner
):
    spaces = lax.axis_size("space")
    device = lax.axis_index("space")
    grid_h = min(8, spaces // 2)
    grid_w = spaces // grid_h
    tok_rows = queries.shape[0]
    head_width = queries.shape[1]
    head_count = head_width // HD
    tile_total = tile_owner.shape[0]
    tile_index = jnp.arange(tile_total, dtype=jnp.int32)
    own_tile = jnp.sum(jnp.where(tile_owner == device, tile_index, 0))
    tile_row = own_tile // grid_w
    tile_col = own_tile % grid_w
    anchor_slot = tile_owner[0]
    right_slot = tile_owner[min(1, tile_total - 1)]
    lower_slot = tile_owner[min(grid_w, tile_total - 1)]
    col_sign = jnp.where(right_slot % grid_w - anchor_slot % grid_w == -1, -1, 1)
    row_sign = jnp.where((lower_slot // grid_w - anchor_slot // grid_w) % grid_h == 1, 1, -1)
    cell_index = jnp.arange(tok_rows, dtype=jnp.int32)
    frame_pos = (cell_index // (TILE * TILE)).astype(jnp.float32)
    height_pos = (tile_row * TILE + cell_index // TILE % TILE).astype(jnp.float32)
    width_pos = (tile_col * TILE + cell_index % TILE).astype(jnp.float32)
    cosine, sine_table = rope_tables(frame_pos, height_pos, width_pos)
    query_rot = rotate(
        queries.astype(jnp.float32).reshape(tok_rows, head_count, HD), cosine, sine_table
    ).astype(jnp.bfloat16)
    key_rot = rotate(
        latent_keys.astype(jnp.float32).reshape(tok_rows, head_count, HD), cosine, sine_table
    ).astype(jnp.bfloat16)
    width_rows = key_weight.shape[0]
    text_cols = lax.dynamic_slice_in_dim(prompt, device * width_rows, width_rows, 1)
    both_weights = jnp.concatenate([key_weight, value_weight], axis=1)
    partial_text = jnp.dot(text_cols, both_weights, preferred_element_type=jnp.float32)
    summed_text = lax.psum(partial_text, "space")
    text_kv = normalize_keys(summed_text, head_count)
    kv_own = jnp.concatenate([key_rot, latent_values], axis=1)
    blocks = []
    valid_parts = []
    for row_step in (-1, 0, 1):
        for col_step in (-1, 0, 1):
            if row_step == 0 and col_step == 0:
                fetched = kv_own
            else:
                fetched = shifted(kv_own, "space", -(row_step * grid_w + col_step))
            near_row = tile_row + row_sign * row_step
            near_col = tile_col + col_sign * col_step
            inside = (near_row >= 0) & (near_row < grid_h) & (near_col >= 0) & (near_col < grid_w)
            blocks.append(fetched)
            valid_parts.append(jnp.zeros((tok_rows,), jnp.int32) + inside.astype(jnp.int32))
    blocks.append(text_kv)
    valid_parts.append(jnp.ones((text_kv.shape[0],), jnp.int32))
    keys_all = jnp.concatenate(blocks, axis=0)
    key_valid = jnp.concatenate(valid_parts, axis=0)
    score_scale = HD ** (-0.5)
    head_outputs = []
    for head_index in range(head_count):
        head_start = head_index * HD
        query_slice = query_rot[:, head_start : head_start + HD]
        key_slice = keys_all[:, head_start : head_start + HD]
        value_slice = keys_all[:, head_width + head_start : head_width + head_start + HD]
        scores = (
            lax.dot_general(
                query_slice, key_slice, (((1,), (1,)), ((), ())), preferred_element_type=jnp.float32
            )
            * score_scale
        )
        scores = jnp.where(key_valid[None, :] > 0, scores, masked_score)
        top_score = jnp.max(scores, axis=-1, keepdims=True)
        exponent = jnp.exp(scores - top_score)
        weights = (exponent / jnp.sum(exponent, axis=-1, keepdims=True)).astype(jnp.bfloat16)
        head_outputs.append(
            jnp.dot(weights, value_slice, preferred_element_type=jnp.float32).astype(jnp.bfloat16)
        )
    attended = jnp.concatenate(head_outputs, axis=1)
    partial_out = jnp.dot(
        attended,
        lax.all_gather(out_weight, "space", axis=1, tiled=True),
        preferred_element_type=jnp.float32,
    )
    summed_out = lax.psum_scatter(
        partial_out.astype(jnp.bfloat16), "heads", scatter_dimension=1, tiled=True
    )
    return summed_out


MESH = pl.DeviceIdType.MESH


UP_AT = 28
DOWN_AT = 31
ACROSS_AT = 34


def mult(value, step):
    return pl.multiple_of(value, step)


def fused_kernel(
    rows,
    tok_rows,
    head_count,
    owner_ref,
    table_ref,
    q_ref,
    k_ref,
    v_ref,
    prompt_ref,
    kw_hbm,
    vw_hbm,
    ow_ref,
    out_ref,
    tcols,
    kw_ref,
    vw_ref,
    padded,
    xs_q,
    xs_kv,
    qbuf,
    kv,
    txs,
    txr,
    tsum,
    near_s,
    near_r,
    far_s,
    far_r,
    att,
    wbuf,
    part_s,
    part_r,
    kept,
    swap_s,
    swap_r,
    local_sem,
    send_sem,
    recv_sem,
):
    g = lax.axis_index("groups")
    s = lax.axis_index("space")
    h = lax.axis_index("heads")
    a, b = s // 2, s % 2
    other = 1 - b
    half = head_count // 2
    width = half * HD
    full = head_count * HD
    x_peer = {"space": a * 2 + other}
    y_peer = {"groups": 1 - g}
    core_peer = {"heads": 1 - h}
    z_peer = [{"space": lax.rem(a + d, 4) * 2 + b} for d in range(4)]
    kdim = kw_hbm.shape[0]
    text = tsum.shape[0]
    piece = text // 4
    text_at = 6 * rows

    fetch = pltpu.make_async_copy(
        prompt_ref.at[:, pl.ds(mult(s * kdim, 128), kdim)], tcols, local_sem.at[0]
    )
    fetches = [
        fetch,
        pltpu.make_async_copy(kw_hbm, kw_ref, local_sem.at[1]),
        pltpu.make_async_copy(vw_hbm, vw_ref, local_sem.at[2]),
    ]
    own_w = pltpu.make_async_copy(
        ow_ref.at[pl.ds(mult(b * width, 16), width)], wbuf.at[s], local_sem.at[3]
    )
    for copy in fetches + [own_w]:
        copy.start()

    barrier = pltpu.get_barrier_semaphore()
    peers = [x_peer, y_peer, core_peer, z_peer[1], z_peer[2], z_peer[3]]
    for peer in peers:
        pl.semaphore_signal(barrier, inc=1, device_id=peer, device_id_type=MESH)

    started = []

    def send(source, target, peer):
        index = len(started)
        copy = pltpu.make_async_remote_copy(
            src_ref=source,
            dst_ref=target,
            send_sem=send_sem.at[index],
            recv_sem=recv_sem.at[index],
            device_id=peer,
            device_id_type=MESH,
        )
        copy.start()
        started.append(copy)
        return copy

    for part, ref in enumerate((q_ref, k_ref, v_ref)):
        place = slice(part * full, (part + 1) * full)
        padded[rows - 16 :, place] = jnp.zeros((16, full), jnp.float32)
        padded[:tok_rows, place] = ref[...].astype(jnp.float32)

    own_tile = jnp.int32(0)
    for t in range(8):
        own_tile = own_tile + jnp.where(owner_ref[t] == s, t, 0)
    first_row, lower_row = owner_ref[0] // 2, owner_ref[2] // 2
    row_sign = jnp.where(lax.rem(lower_row - first_row + 4, 4) == 1, 1, -1)
    tile_row = own_tile // 2
    one_hot = lax.broadcasted_iota(jnp.int32, (8, HD), 0) == own_tile
    shift_cos, shift_sin = [
        jnp.sum(
            jnp.where(one_hot, table_ref[2 * rows + 8 * k : 2 * rows + 8 * k + 8], 0.0),
            axis=0,
            keepdims=True,
        )
        for k in range(2)
    ]
    base_cos, base_sin = table_ref[:rows], table_ref[rows : 2 * rows]
    even = lax.broadcasted_iota(jnp.int32, (rows, HD), 1) % 2 == 0
    cosine = base_cos * shift_cos - base_sin * shift_sin
    sine = base_sin * shift_cos + base_cos * shift_sin
    sine = jnp.where(even, -sine, sine)

    def turned(column):
        x = padded[:, pl.ds(mult(column, 128), HD)]
        swapped = jnp.where(even, pltpu.roll(x, HD - 1, 1), pltpu.roll(x, 1, 1))
        return (x * cosine + swapped * sine).astype(jnp.bfloat16)

    def seg(row, tile):
        return pl.ds(mult((row * 2 + tile) * rows, 16), rows)

    for m in range(half):
        place = slice(m * HD, (m + 1) * HD)
        xs_kv[:, place] = turned(full + other * width + m * HD)
        xs_q[:, place] = turned(other * width + m * HD)
        kv[seg(0, b), place] = turned(full + b * width + m * HD)
    xs_kv[:, width:] = padded[:, pl.ds(mult(2 * full + other * width, 128), width)].astype(jnp.bfloat16)
    kv[seg(0, b), width:] = padded[:, pl.ds(mult(2 * full + b * width, 128), width)].astype(jnp.bfloat16)

    pl.semaphore_wait(barrier, len(peers))

    def text_part(which):
        cols = pl.ds(mult(which * width, 128), width)
        return [
            jnp.dot(tcols[...], w[:, cols], preferred_element_type=jnp.float32)
            for w in (kw_ref, vw_ref)
        ]

    x_kv = send(xs_kv, kv.at[seg(0, b)], x_peer)
    z_kv = [
        send(kv.at[seg(0, b)], kv.at[seg(1, b)], z_peer[1]),
        send(kv.at[seg(0, b)], kv.at[seg(2, b)], z_peer[3]),
    ]
    for copy in fetches:
        copy.wait()
    key_part, value_part = text_part(other)
    txs[:, :width] = key_part.astype(jnp.bfloat16)
    txs[:, width:] = value_part.astype(jnp.bfloat16)
    x_text = send(txs, txr, x_peer)
    x_w = send(
        ow_ref.at[pl.ds(mult(other * width, 16), width)], wbuf.at[s], x_peer
    )

    x_q = send(xs_q, qbuf.at[b], x_peer)
    key_part, value_part = text_part(b)
    tsum[:, :width] = key_part
    tsum[:, width:] = value_part
    for m in range(half):
        qbuf[b, :, m * HD : (m + 1) * HD] = turned(b * width + m * HD)
    own_w.wait()

    x_kv.wait_recv()
    z_kv += [
        send(kv.at[seg(0, other)], kv.at[seg(1, other)], z_peer[1]),
        send(kv.at[seg(0, other)], kv.at[seg(2, other)], z_peer[3]),
    ]

    sub = width // 2
    mine = pl.ds(mult(g * sub, 16), sub)

    def row_of_chunks(row):
        return wbuf.at[pl.ds(row * 2, 2), mine]

    def copy_at(index, view, peer):
        return pltpu.make_async_remote_copy(
            src_ref=view,
            dst_ref=view,
            send_sem=send_sem.at[index],
            recv_sem=recv_sem.at[index],
            device_id=peer,
            device_id_type=MESH,
        )

    up_peer = {"space": jnp.minimum(a + 1, 3) * 2 + b}
    down_peer = {"space": jnp.maximum(a - 1, 0) * 2 + b}

    def up_copy(k):
        return copy_at(UP_AT + k, row_of_chunks(jnp.maximum(a - k, 0)), up_peer)

    def down_copy(k):
        return copy_at(DOWN_AT + k, row_of_chunks(jnp.minimum(a + k, 3)), down_peer)

    def across_copy(d):
        return copy_at(ACROSS_AT + d, row_of_chunks(lax.rem(a + d, 4)), y_peer)

    def relay(k):
        @pl.when(a >= k + 1)
        def _():
            up_copy(k).wait_recv()
            across_copy(3 - k).start()

        if k < 2:
            @pl.when((a >= k + 1) & (a < 3))
            def _():
                up_copy(k + 1).start()

        @pl.when(a <= 2 - k)
        def _():
            down_copy(k).wait_recv()
            across_copy(1 + k).start()

        if k < 2:
            @pl.when((a <= 2 - k) & (a > 0))
            def _():
                down_copy(k + 1).start()

    x_text.wait_recv()
    parity, upper = a % 2, a // 2
    pair = 2 * piece
    near_peer = {"space": (a + 1 - 2 * parity) * 2 + b}
    far_peer = {"space": lax.rem(a + 2, 4) * 2 + b}
    block = pl.ds(mult((1 - parity) * pair, 16), pair)
    near_s[...] = (tsum[block, :] + txr[block, :].astype(jnp.float32)).astype(jnp.bfloat16)
    near_text = send(near_s, near_r, near_peer)
    block = pl.ds(mult(parity * pair, 16), pair)
    tsum[block, :] = tsum[block, :] + txr[block, :].astype(jnp.float32)

    x_w.wait_recv()

    @pl.when(a < 3)
    def _():
        up_copy(0).start()

    @pl.when(a > 0)
    def _():
        down_copy(0).start()

    near_text.wait_recv()
    lower_half = pl.ds(mult((1 - upper) * piece, 16), piece)
    block = pl.ds(mult(parity * pair + (1 - upper) * piece, 16), piece)
    far_s[...] = (tsum[block, :] + near_r[lower_half, :].astype(jnp.float32)).astype(jnp.bfloat16)
    far_text = send(far_s, far_r, far_peer)
    kept_half = pl.ds(mult(upper * piece, 16), piece)
    block = pl.ds(mult(parity * pair + upper * piece, 16), piece)
    total = tsum[block, :] + near_r[kept_half, :].astype(jnp.float32)
    far_text.wait_recv()
    total = total + far_r[...].astype(jnp.float32)
    own_text = pl.ds(mult(text_at + parity * pair + upper * piece, 16), piece)
    far_rows = pl.ds(mult(text_at + parity * pair + (1 - upper) * piece, 16), piece)
    for m in range(half):
        x = total[:, m * HD : (m + 1) * HD]
        x = x * lax.rsqrt(jnp.mean(x * x, axis=-1, keepdims=True) + eps_norm)
        kv[own_text, m * HD : (m + 1) * HD] = x.astype(jnp.bfloat16)
    kv[own_text, width:] = total[:, width:].astype(jnp.bfloat16)
    far_kv = send(kv.at[own_text], kv.at[own_text], far_peer)
    near_kv = send(kv.at[own_text], kv.at[own_text], near_peer)
    far_kv.wait_recv()
    near_kv2 = send(kv.at[far_rows], kv.at[far_rows], near_peer)

    relay(0)
    relay(1)
    z_text_kv = [near_kv, near_kv2]
    for copy in [x_q] + z_kv + z_text_kv:
        copy.wait_recv()

    key_at = lax.broadcasted_iota(jnp.int32, (1, kv.shape[0]), 1)
    bias = jnp.where(key_at >= text_at, 0.0, masked_score)
    for row, step in enumerate((0, -1, 1)):
        near = tile_row + row_sign * step
        level = jnp.where((near >= 0) & (near < 4), 0.0, masked_score)
        for tile in range(2):
            low = (row * 2 + tile) * rows
            bias = jnp.where((key_at >= low) & (key_at < low + tok_rows), level, bias)
    for tile in (other, b):
        for m in range(half):
            place = slice(m * HD, (m + 1) * HD)
            scores = lax.dot_general(
                qbuf[tile, :, place],
                kv[:, place],
                (((1,), (1,)), ((), ())),
                preferred_element_type=jnp.float32,
            )
            scores = scores * HD ** (-0.5) + bias
            top = jnp.max(scores, axis=-1, keepdims=True)
            grown = jnp.exp(scores - top)
            scaled = grown * (1.0 / jnp.sum(grown, axis=-1, keepdims=True))
            result = jnp.dot(
                scaled.astype(jnp.bfloat16),
                kv[:, width + m * HD : width + (m + 1) * HD],
                preferred_element_type=jnp.float32,
            ).astype(jnp.bfloat16)
            att[pl.ds(mult(tile * rows, 16), rows), place] = result
        if tile is other:
            relay(2)

    for d in (1, 2, 3):
        across_copy(d).wait_recv()
    cols = wbuf.shape[2]
    core = []
    for j in range(4):
        part_s[j] = jnp.dot(
            att[...], wbuf[(1 - h) * 4 + j], preferred_element_type=jnp.float32
        ).astype(jnp.bfloat16)
        core.append(send(part_s.at[j], part_r.at[j], core_peer))
    for j in range(4):
        kept[j] = jnp.dot(att[...], wbuf[h * 4 + j], preferred_element_type=jnp.float32)
    sent_rows = pl.ds(mult(other * rows, 16), rows)
    own_rows = pl.ds(mult(b * rows, 16), rows)
    swap = []
    for j in range(4):
        core[j].wait_recv()
        swap_s[j] = (
            kept[j, sent_rows, :] + part_r[j, sent_rows, :].astype(jnp.float32)
        ).astype(jnp.bfloat16)
        swap.append(send(swap_s.at[j], swap_r.at[j], x_peer))
    for j in range(4):
        total = kept[j, own_rows, :] + part_r[j, own_rows, :].astype(jnp.float32)
        swap[j].wait_recv()
        out_ref[:, j * cols : (j + 1) * cols] = (
            total + swap_r[j].astype(jnp.float32)
        ).astype(jnp.bfloat16)

    for copy in started:
        copy.wait_send()
    for d in (1, 2, 3):
        across_copy(d).wait_send()
    for k in range(3):
        @pl.when((a >= k) & (a < 3))
        def _():
            up_copy(k).wait_send()

        @pl.when((a <= 3 - k) & (a > 0))
        def _():
            down_copy(k).wait_send()


def rope_constants(rows):
    pair = np.arange(HD) // 2
    first = RT // 2
    second = first + RH // 2
    in_height = (pair >= first) & (pair < second)
    time = np.where(pair < first, rope_theta ** (-2.0 * pair / RT), 0.0)
    height = np.where(in_height, rope_theta ** (-2.0 * (pair - first) / RH), 0.0)
    width = np.where(pair >= second, rope_theta ** (-2.0 * (pair - second) / RH), 0.0)
    cell = np.arange(rows)[:, None]
    base = cell // (TILE * TILE) * time + cell // TILE % TILE * height + cell % TILE * width
    tile = np.arange(8)[:, None]
    shift = tile // 2 * TILE * height + tile % 2 * TILE * width
    tables = [np.cos(base), np.sin(base), np.cos(shift), np.sin(shift)]
    return np.concatenate(tables).astype(np.float32)


def fused_body(
    queries, latent_keys, latent_values, prompt, key_weight, value_weight, out_weight, tile_owner
):
    tok_rows = queries.shape[0]
    full = queries.shape[1]
    head_count = full // HD
    width = full // 2
    text = prompt.shape[0]
    rows = -(-tok_rows // 16) * 16
    keys = 6 * rows + text
    chunk = out_weight.shape
    bf16 = jnp.bfloat16
    vmem = pl.BlockSpec(memory_space=pltpu.VMEM)
    smem = pl.BlockSpec(memory_space=pltpu.SMEM)
    hbm = pl.BlockSpec(memory_space=pltpu.HBM)
    copies = 40
    result = pl.pallas_call(
        functools.partial(fused_kernel, rows, tok_rows, head_count),
        out_shape=jax.ShapeDtypeStruct((rows, 4 * chunk[1]), bf16),
        in_specs=[smem, vmem, vmem, vmem, vmem, hbm, hbm, hbm, hbm],
        out_specs=vmem,
        scratch_shapes=[
            pltpu.VMEM((text, key_weight.shape[0]), bf16),
            pltpu.VMEM(key_weight.shape, bf16),
            pltpu.VMEM(key_weight.shape, bf16),
            pltpu.VMEM((rows, 3 * full), jnp.float32),
            pltpu.VMEM((rows, width), bf16),
            pltpu.VMEM((rows, full), bf16),
            pltpu.VMEM((2, rows, width), bf16),
            pltpu.VMEM((keys, full), bf16),
            pltpu.VMEM((text, full), bf16),
            pltpu.VMEM((text, full), bf16),
            pltpu.VMEM((text, full), jnp.float32),
            pltpu.VMEM((text // 2, full), bf16),
            pltpu.VMEM((text // 2, full), bf16),
            pltpu.VMEM((text // 4, full), bf16),
            pltpu.VMEM((text // 4, full), bf16),
            pltpu.VMEM((2 * rows, width), bf16),
            pltpu.VMEM((8, width, chunk[1]), bf16),
            pltpu.VMEM((4, 2 * rows, chunk[1]), bf16),
            pltpu.VMEM((4, 2 * rows, chunk[1]), bf16),
            pltpu.VMEM((4, 2 * rows, chunk[1]), jnp.float32),
            pltpu.VMEM((4, rows, chunk[1]), bf16),
            pltpu.VMEM((4, rows, chunk[1]), bf16),
            pltpu.SemaphoreType.DMA((4,)),
            pltpu.SemaphoreType.DMA((copies,)),
            pltpu.SemaphoreType.DMA((copies,)),
        ],
        compiler_params=pltpu.CompilerParams(
            collective_id=0, has_side_effects=True, vmem_limit_bytes=60 * 1024 * 1024
        ),
    )(
        tile_owner,
        rope_constants(rows),
        queries,
        latent_keys,
        latent_values,
        prompt,
        key_weight,
        value_weight,
        out_weight,
    )
    return result[:tok_rows]


def solution(mesh):
    in_specs = (
        P(("groups", "space"), "heads"),
        P(("groups", "space"), "heads"),
        P(("groups", "space"), "heads"),
        P("groups", None),
        P("space", "heads"),
        P("space", "heads"),
        P("heads", "space"),
        P("groups"),
    )
    out_specs = P(("groups", "space"), "heads")
    small = mesh.shape["space"] == 8 and mesh.shape["groups"] == 2 and mesh.shape["heads"] == 2
    chosen = fused_body if small else body
    return jax.shard_map(chosen, mesh=mesh, in_specs=in_specs, out_specs=out_specs, check_vma=False)
```
